512 devices in a mesh: dp: 8 (over z_lo, x), row: 8 (over z_hi, core), col: 8 (over y).
Axes of the slice: x: 4, y: 8, z: 8 (z_hi: 4, z_lo: 2; z = z_hi * 2 + z_lo), core: 2. Of those that a mesh axis runs over, the one named last changes fastest.
Arguments:
- inputs: bfloat16 [256, 16384], P(('dp', 'col'), 'row'), may hold values from -6 to 6
- cotangent: bfloat16 [256, 16384], P(('dp', 'col'), 'row'), may hold values from -3 to 3
- gate_weight: bfloat16 [16384, 8192], P('row', ('dp', 'col')), may hold values from -0.046875 to 0.046875
- up_weight: bfloat16 [16384, 8192], P('row', ('dp', 'col')), may hold values from -0.046875 to 0.046875
- down_weight: bfloat16 [8192, 16384], P(('dp', 'col'), 'row'), may hold values from -0.0625 to 0.0625
Outputs:
- grad_inputs: bfloat16 [256, 16384], P(('dp', 'col'), 'row')
- grad_gate_weight: bfloat16 [16384, 8192], P('row', ('dp', 'col'))
- grad_up_weight: bfloat16 [16384, 8192], P('row', ('dp', 'col'))
- grad_down_weight: bfloat16 [8192, 16384], P(('dp', 'col'), 'row')
The draws below stay inside these ranges and needn't reach their ends.
All inputs are finite; a program needn't handle non-finite values.
Results may differ from the reference program's by a relative error of at most 0.0049.
Values may be sent and summed in bfloat16 or wider, within the bound.
No kernel may reach another device: no remote copies, remote signals or barrier semaphores. Data moves between devices by JAX's collectives and lax.ppermute only.
A program may use at most 64 MiB of HBM per device.

```python
import jax
import jax.numpy as jnp

D = 16384
F = 8192
TOKENS = 256


def steps_of(key, shape, cuts, least, top_value):
    def one(axis_at, blocks):
        draws = jax.random.uniform(jax.random.fold_in(jax.random.fold_in(key, 6), axis_at), (blocks,), jnp.float32, least / len(cuts), top_value / len(cuts))
        return jnp.repeat(jnp.exp(draws), shape[axis_at] // blocks).reshape((-1,) + (1,) * (len(shape) - axis_at - 1))

    gain = one(*cuts[0])
    for cut in cuts[1:]:
        gain = gain * one(*cut)
    return gain


def normal_values(stream_key, shape, deviation, most, cuts=(), held_as=jnp.bfloat16):
    values = jax.random.normal(stream_key, shape, jnp.float32) * deviation
    if len(cuts) > 0:
        values = steps_of(stream_key, shape, cuts, -0.22, 0.18) * values
    return jnp.clip(values, min=-most, max=most).astype(held_as)


def setup_inputs(seed: int = 0) -> dict:
    seeds = jax.random.split(jax.random.key(seed), 6)
    inputs = normal_values(seeds[0], (TOKENS, D), 1.0, 6.0, ((0, 64), (1, 8)))
    cotangent = normal_values(seeds[1], (TOKENS, D), 0.3, 3.0, ((0, 64), (1, 8)))
    gate_weight = normal_values(seeds[2], (D, F), D ** -0.5, 0.046875, ((0, 8), (1, 64)))
    up_weight = normal_values(seeds[3], (D, F), D ** -0.5, 0.046875, ((0, 8), (1, 64)))
    down_weight = normal_values(seeds[4], (F, D), F ** -0.5, 0.0625, ((0, 64), (1, 8)))
    return dict(inputs=inputs, cotangent=cotangent, gate_weight=gate_weight, up_weight=up_weight, down_weight=down_weight)


def reference(inputs, cotangent, gate_weight, up_weight, down_weight):
    gate = jnp.dot(inputs, gate_weight, preferred_element_type=jnp.float32)
    up = jnp.dot(inputs, up_weight, preferred_element_type=jnp.float32)
    hidden_grad = jnp.dot(cotangent, down_weight.T, preferred_element_type=jnp.float32)
    sigma = jax.nn.sigmoid(gate)
    active = gate * sigma
    hidden = (active * up).astype(jnp.bfloat16)
    up_grad = (hidden_grad * active).astype(jnp.bfloat16)
    gate_grad = (hidden_grad * up * sigma * (1.0 + gate * (1.0 - sigma))).astype(jnp.bfloat16)
    grad_inputs = (jnp.dot(gate_grad, gate_weight.T, preferred_element_type=jnp.float32)
                   + jnp.dot(up_grad, up_weight.T, preferred_element_type=jnp.float32)).astype(jnp.bfloat16)
    grad_gate_weight = jnp.dot(inputs.T, gate_grad, preferred_element_type=jnp.float32).astype(jnp.bfloat16)
    grad_up_weight = jnp.dot(inputs.T, up_grad, preferred_element_type=jnp.float32).astype(jnp.bfloat16)
    grad_down_weight = jnp.dot(hidden.T, cotangent, preferred_element_type=jnp.float32).astype(jnp.bfloat16)
    return grad_inputs, grad_gate_weight, grad_up_weight, grad_down_weight
```

```python
import jax
import jax.numpy as jnp
from jax import lax
from jax.sharding import PartitionSpec as P

GROUP = ("dp", "col")


def gather_rows(block, axes):
    n = lax.axis_size(axes)
    copies = jnp.broadcast_to(block[None], (n,) + block.shape)
    return lax.all_to_all(copies, axes, split_axis=0, concat_axis=0, tiled=True)


def swiglu_grads(summed, width):
    gate = summed[:, :width]
    up = summed[:, width : 2 * width]
    hidden_grad = summed[:, 2 * width :]
    sigma = jax.nn.sigmoid(gate)
    active = gate * sigma
    hidden = (active * up).astype(jnp.bfloat16)
    up_grad = (hidden_grad * active).astype(jnp.bfloat16)
    gate_grad = (hidden_grad * up * sigma * (1.0 + gate * (1.0 - sigma))).astype(jnp.bfloat16)
    return (hidden, gate_grad, up_grad)


def body(inputs, cotangent, gate_weight, up_weight, down_weight):
    depth, width = gate_weight.shape
    groups = lax.axis_size(GROUP)
    rows = lax.axis_size("row")
    tokens = inputs.shape[0] * groups
    gathered_in = gather_rows(inputs, GROUP).reshape(tokens, depth)
    gathered_cot = gather_rows(cotangent, GROUP).reshape(tokens, depth)
    joined = jnp.concatenate([gate_weight, up_weight], axis=1)
    forward = jnp.dot(gathered_in, joined, preferred_element_type=jnp.float32)
    backward = lax.dot_general(
        gathered_cot, down_weight, (((1,), (1,)), ((), ())), preferred_element_type=jnp.float32
    )
    partial = jnp.concatenate([forward, backward], axis=1).reshape(rows, tokens // rows, 3 * width)
    summed = jnp.sum(lax.all_to_all(partial, "row", split_axis=0, concat_axis=0, tiled=True), axis=0)
    triple = jnp.concatenate(swiglu_grads(summed, width), axis=1)
    triple = lax.all_gather(triple, "row", axis=0, tiled=True)
    hidden = triple[:, :width]
    both_grads = triple[:, width:]
    partial_in = lax.dot_general(
        both_grads, joined, (((1,), (1,)), ((), ())), preferred_element_type=jnp.float32
    ).astype(jnp.bfloat16)
    pieces = lax.all_to_all(
        partial_in.reshape(groups, tokens // groups, depth), GROUP, split_axis=0, concat_axis=0, tiled=True
    )
    grad_inputs = jnp.sum(pieces.astype(jnp.float32), axis=0).astype(jnp.bfloat16)
    contract_rows = (((0,), (0,)), ((), ()))
    grad_gate_weight = lax.dot_general(
        gathered_in, both_grads[:, :width], contract_rows, preferred_element_type=jnp.float32
    ).astype(jnp.bfloat16)
    grad_up_weight = lax.dot_general(
        gathered_in, both_grads[:, width:], contract_rows, preferred_element_type=jnp.float32
    ).astype(jnp.bfloat16)
    grad_down_weight = lax.dot_general(
        hidden, gathered_cot, contract_rows, preferred_element_type=jnp.float32
    ).astype(jnp.bfloat16)
    return (grad_inputs, grad_gate_weight, grad_up_weight, grad_down_weight)


def solution(mesh):
    in_specs = (
        P(("dp", "col"), "row"),
        P(("dp", "col"), "row"),
        P("row", ("dp", "col")),
        P("row", ("dp", "col")),
        P(("dp", "col"), "row"),
    )
    out_specs = (
        P(("dp", "col"), "row"),
        P("row", ("dp", "col")),
        P("row", ("dp", "col")),
        P(("dp", "col"), "row"),
    )
    return jax.shard_map(body, mesh=mesh, in_specs=in_specs, out_specs=out_specs, check_vma=False)
```

```python
import jax
import jax.numpy as jnp
from jax import lax
from jax.sharding import Mesh
from jax.sharding import PartitionSpec as P

DP = ("z_lo", "x")
GROUP = ("z_lo", "x", "col")
ROW = ("z_hi", "core")


def exchange(pieces, axes):
    return lax.all_to_all(pieces, axes, split_axis=0, concat_axis=0, tiled=True)


def spread(block, axes):
    n = lax.axis_size(axes)
    return exchange(jnp.broadcast_to(block[None], (n,) + block.shape), axes)


def swiglu_grads(summed, width):
    gate = summed[:, :width]
    up = summed[:, width : 2 * width]
    hidden_grad = summed[:, 2 * width :]
    sigma = jax.nn.sigmoid(gate)
    active = gate * sigma
    hidden = (active * up).astype(jnp.bfloat16)
    up_grad = (hidden_grad * active).astype(jnp.bfloat16)
    gate_grad = (hidden_grad * up * sigma * (1.0 + gate * (1.0 - sigma))).astype(jnp.bfloat16)
    return (hidden, gate_grad, up_grad)


def body(inputs, cotangent, gate_weight, up_weight, down_weight):
    own, depth = inputs.shape
    width = gate_weight.shape[1]
    columns = lax.axis_size("col")
    planes = lax.axis_size(DP)
    groups = columns * planes
    tokens = own * groups

    line = spread(jnp.concatenate([inputs, cotangent], axis=0), "col")
    line = line.reshape(columns, 2, own, depth).transpose(1, 0, 2, 3).reshape(2 * columns * own, depth)
    plane = spread(line, DP).reshape(planes, 2, columns * own, depth)
    gathered_in = plane[:, 0].reshape(tokens, depth)
    gathered_cot = plane[:, 1].reshape(tokens, depth)

    joined = jnp.concatenate([gate_weight, up_weight], axis=1)
    forward = jnp.dot(gathered_in, joined, preferred_element_type=jnp.float32)
    backward = lax.dot_general(
        gathered_cot, down_weight, (((1,), (1,)), ((), ())), preferred_element_type=jnp.float32
    )
    halves = jnp.concatenate([forward, backward], axis=1).reshape(2, tokens // 2, 3 * width)
    core = lax.axis_index("core")
    mine = lax.dynamic_index_in_dim(halves, core, 0, keepdims=False)
    other = lax.dynamic_index_in_dim(halves, 1 - core, 0, keepdims=False)
    pair = mine + lax.ppermute(other, "core", [(0, 1), (1, 0)])
    summed = jnp.sum(spread(pair, "z_hi"), axis=0)
    triple = jnp.concatenate(swiglu_grads(summed, width), axis=1)
    triple = lax.all_gather(triple, "core", axis=0, tiled=True)
    hidden = triple[:, :width]
    both_grads = triple[:, width:]

    partial_in = lax.dot_general(
        both_grads, joined, (((1,), (1,)), ((), ())), preferred_element_type=jnp.float32
    ).astype(jnp.bfloat16)
    pieces = exchange(partial_in.reshape(groups, own, depth), GROUP)
    grad_inputs = jnp.sum(pieces.astype(jnp.float32), axis=0).astype(jnp.bfloat16)
    contract_rows = (((0,), (0,)), ((), ()))
    grad_gate_weight = lax.dot_general(
        gathered_in, both_grads[:, :width], contract_rows, preferred_element_type=jnp.float32
    ).astype(jnp.bfloat16)
    grad_up_weight = lax.dot_general(
        gathered_in, both_grads[:, width:], contract_rows, preferred_element_type=jnp.float32
    ).astype(jnp.bfloat16)
    grad_down_weight = lax.dot_general(
        hidden, gathered_cot, contract_rows, preferred_element_type=jnp.float32
    ).astype(jnp.bfloat16)
    return (grad_inputs, grad_gate_weight, grad_up_weight, grad_down_weight)


def solution(mesh):
    fine = Mesh(mesh.devices.reshape(2, 4, 4, 2, 8), ("z_lo", "x", "z_hi", "core", "col"))
    in_specs = (P(GROUP, ROW), P(GROUP, ROW), P(ROW, GROUP), P(ROW, GROUP), P(GROUP, ROW))
    out_specs = (P(GROUP, ROW), P(ROW, GROUP), P(ROW, GROUP), P(GROUP, ROW))
    return jax.shard_map(body, mesh=fine, in_specs=in_specs, out_specs=out_specs, check_vma=False)
```

```python
import functools

import jax
import jax.numpy as jnp
from jax import lax
from jax.experimental import pallas as pl
from jax.experimental.pallas import tpu as pltpu
from jax.sharding import Mesh
from jax.sharding import PartitionSpec as P

DP = ("z_lo", "x")
GROUP = ("z_lo", "x", "col")
ROW = ("z_hi", "core")
LIMIT = 40 * 1024 * 1024
F32 = jnp.float32
BF16 = jnp.bfloat16
LAST = (((1,), (1,)), ((), ()))
FIRST = (((0,), (0,)), ((), ()))


def exchange(pieces, axes):
    return lax.all_to_all(pieces, axes, split_axis=0, concat_axis=0, tiled=True)


def spread(block, axes):
    n = lax.axis_size(axes)
    return exchange(jnp.broadcast_to(block[None], (n,) + block.shape), axes)


def call(kernel, out_shape, cost, **rest):
    flops, size = cost
    return pl.pallas_call(
        kernel,
        out_shape=out_shape,
        cost_estimate=pl.CostEstimate(flops=flops, bytes_accessed=size, transcendentals=0),
        compiler_params=pltpu.CompilerParams(vmem_limit_bytes=LIMIT),
        **rest,
    )


def upper(shape):
    return lax.broadcasted_iota(jnp.int32, shape, len(shape) - 2) < 4


def split_line(line_ref, out_ref, kept, sems):
    columns, _, depth = line_ref.shape
    blocks = line_ref[...].astype(F32)
    top = upper((8, depth))
    inputs, cotangents = [], []
    for j in range(columns // 2):
        a, b = blocks[2 * j], blocks[2 * j + 1]
        inputs.append(jnp.where(top, a, pltpu.roll(b, 4, 0)))
        cotangents.append(jnp.where(top, pltpu.roll(a, 4, 0), b))
    kept[...] = jnp.concatenate(inputs + cotangents, axis=0).astype(BF16)
    copies = [pltpu.make_async_copy(kept, out_ref.at[p], sems.at[p]) for p in range(out_ref.shape[0])]
    for copy in copies:
        copy.start()
    for copy in copies:
        copy.wait()


def forward(which_ref, plane_ref, gate_ref, up_ref, down_ref, out_ref):
    planes, rows, depth = plane_ref.shape
    half = rows // 2
    width = gate_ref.shape[1]
    inputs = plane_ref[:, :half, :].reshape(planes * half, depth)
    cotangents = plane_ref[:, half:, :].reshape(planes * half, depth)
    joined = jnp.concatenate([gate_ref[...], up_ref[...]], axis=1)
    out_ref[:, : 2 * width] = jnp.dot(inputs, joined, preferred_element_type=F32)
    out_ref[:, 2 * width :] = lax.dot_general(cotangents, down_ref[...], LAST, preferred_element_type=F32)


def run_forward(which, plane, gate_weight, up_weight, down_weight):
    planes, rows, depth = plane.shape
    width = gate_weight.shape[1]
    tokens = planes * rows // 4
    whole = lambda i, c: (0, 0)
    return call(
        forward,
        jax.ShapeDtypeStruct((tokens, 3 * width), F32),
        (6 * tokens * depth * width, plane.size + 6 * depth * width),
        grid_spec=pltpu.PrefetchScalarGridSpec(
            num_scalar_prefetch=1,
            grid=(1,),
            in_specs=[
                pl.BlockSpec((planes // 2, rows, depth), lambda i, c: (c[0], 0, 0)),
                pl.BlockSpec(gate_weight.shape, whole),
                pl.BlockSpec(up_weight.shape, whole),
                pl.BlockSpec(down_weight.shape, whole),
            ],
            out_specs=pl.BlockSpec((tokens, 3 * width), whole),
        ),
    )(which, plane, gate_weight, up_weight, down_weight)


def activate(parts_ref, out_ref):
    width = out_ref.shape[1] // 3
    summed = jnp.sum(parts_ref[...], axis=0)
    gate = summed[:, :width]
    up = summed[:, width : 2 * width]
    hidden_grad = summed[:, 2 * width :]
    sigma = 1.0 / (1.0 + jnp.exp(-gate))
    active = gate * sigma
    out_ref[:, :width] = (active * up).astype(BF16)
    out_ref[:, width : 2 * width] = (hidden_grad * up * sigma * (1.0 + gate * (1.0 - sigma))).astype(BF16)
    out_ref[:, 2 * width :] = (hidden_grad * active).astype(BF16)


def input_grads(triple_ref, gate_ref, up_ref, out_ref):
    tokens = triple_ref.shape[0]
    width = gate_ref.shape[1]
    depth = gate_ref.shape[0]
    both = triple_ref[:, width:]
    step = 256
    top = upper((tokens // 8, 8, step))
    for n in range(0, depth // 2, step):
        sides = []
        for at in (n, depth // 2 + n):
            joined = jnp.concatenate([gate_ref[at : at + step, :], up_ref[at : at + step, :]], axis=1)
            product = lax.dot_general(both, joined, LAST, preferred_element_type=F32)
            sides.append(product.reshape(tokens // 8, 8, step))
        left, right = sides
        out_ref[:, 0, :, n : n + step] = jnp.where(top, left, pltpu.roll(right, 4, 1)).astype(BF16)
        out_ref[:, 1, :, n : n + step] = jnp.where(top, pltpu.roll(left, 4, 1), right).astype(BF16)


def add_pieces(pieces_ref, out_ref):
    half = pieces_ref.shape[2]
    total = jnp.sum(pieces_ref[...].astype(F32), axis=0)
    out_ref[:, :half] = total[:4].astype(BF16)
    out_ref[:, half:] = pltpu.roll(total, 4, 0)[:4].astype(BF16)


def body(inputs, cotangent, gate_weight, up_weight, down_weight):
    own, depth = inputs.shape
    width = gate_weight.shape[1]
    columns = lax.axis_size("col")
    planes = lax.axis_size(DP)
    groups = columns * planes
    tokens = own * groups
    rows = 2 * columns * own
    shape = jax.ShapeDtypeStruct

    line = spread(jnp.concatenate([inputs, cotangent], axis=0), "col").reshape(columns, 2 * own, depth)
    copies = call(
        split_line,
        shape((planes, rows, depth), BF16),
        (0, planes * rows * depth * 2),
        out_specs=pl.BlockSpec(memory_space=pltpu.HBM),
        scratch_shapes=[pltpu.VMEM((rows, depth), BF16), pltpu.SemaphoreType.DMA((planes,))],
    )(line)
    plane = exchange(copies, DP).reshape(planes, rows, depth)

    core = lax.axis_index("core").astype(jnp.int32).reshape(1)
    other = run_forward(1 - core, plane, gate_weight, up_weight, down_weight)
    swapped = lax.ppermute(other, "core", [(0, 1), (1, 0)])
    mine = run_forward(core, plane, gate_weight, up_weight, down_weight)
    pair = mine + swapped

    pair, later = lax.optimization_barrier((pair, plane))
    parts = spread(pair, "z_hi").reshape(lax.axis_size("z_hi"), tokens // 2, 3 * width)
    gathered_in = later[:, : rows // 2].reshape(tokens, depth)
    gathered_cot = later[:, rows // 2 :].reshape(tokens, depth)
    parts, gathered_in, gathered_cot = lax.optimization_barrier((parts, gathered_in, gathered_cot))

    triple = call(activate, shape((tokens // 2, 3 * width), BF16), (tokens * width * 10, parts.size * 4))(parts)
    triple = lax.all_gather(triple, "core", axis=0, tiled=True)

    partial_in = call(
        input_grads,
        shape((groups // 2, 2, 2 * own, depth // 2), BF16),
        (4 * tokens * depth * width, 2 * tokens * depth + 4 * depth * width),
    )(triple, gate_weight, up_weight)
    pieces = exchange(partial_in.reshape(groups, 2 * own, depth // 2), GROUP)
    grad_inputs = call(add_pieces, shape((own, depth), BF16), (tokens * depth, 2 * tokens * depth))(pieces)

    hidden, gate_grad, up_grad = (triple[:, i * width : (i + 1) * width] for i in range(3))
    product = functools.partial(lax.dot_general, dimension_numbers=FIRST, preferred_element_type=F32)
    grad_gate_weight = product(gathered_in, gate_grad).astype(BF16)
    grad_up_weight = product(gathered_in, up_grad).astype(BF16)
    grad_down_weight = product(hidden, gathered_cot).astype(BF16)
    return (grad_inputs, grad_gate_weight, grad_up_weight, grad_down_weight)


def solution(mesh):
    fine = Mesh(mesh.devices.reshape(2, 4, 4, 2, 8), ("z_lo", "x", "z_hi", "core", "col"))
    in_specs = (P(GROUP, ROW), P(GROUP, ROW), P(ROW, GROUP), P(ROW, GROUP), P(GROUP, ROW))
    out_specs = (P(GROUP, ROW), P(ROW, GROUP), P(ROW, GROUP), P(GROUP, ROW))
    return jax.shard_map(body, mesh=fine, in_specs=in_specs, out_specs=out_specs, check_vma=False)
```

```python
import functools

import jax
import jax.numpy as jnp
from jax import lax
from jax.experimental import pallas as pl
from jax.experimental.pallas import tpu as pltpu
from jax.sharding import Mesh
from jax.sharding import PartitionSpec as P

DP = ("z_lo", "x")
GROUP = ("z_lo", "x", "col")
ROW = ("z_hi", "core")
MIB = 1024 * 1024
EXTRA = 16
TOP = 14
F16 = jnp.float16
F32 = jnp.float32
BF16 = jnp.bfloat16
LAST = (((1,), (1,)), ((), ()))
FIRST = (((0,), (0,)), ((), ()))


def exchange(pieces, axes):
    return lax.all_to_all(pieces, axes, split_axis=0, concat_axis=0, tiled=True)


def spread(block, axes):
    n = lax.axis_size(axes)
    return exchange(jnp.broadcast_to(block[None], (n,) + block.shape), axes)


def call(kernel, out_shape, cost, limit=20, **rest):
    flops, size = cost
    return pl.pallas_call(
        kernel,
        out_shape=out_shape,
        cost_estimate=pl.CostEstimate(flops=flops, bytes_accessed=size, transcendentals=0),
        compiler_params=pltpu.CompilerParams(vmem_limit_bytes=limit * MIB),
        **rest,
    )


def upper(shape):
    return lax.broadcasted_iota(jnp.int32, shape, len(shape) - 2) < 4


def split_line(line_ref, out_ref, kept, sems):
    columns, _, depth = line_ref.shape
    blocks = line_ref[...].astype(F32)
    top = upper((8, depth))
    inputs, cotangents = [], []
    for j in range(columns // 2):
        a, b = blocks[2 * j], blocks[2 * j + 1]
        inputs.append(jnp.where(top, a, pltpu.roll(b, 4, 0)))
        cotangents.append(jnp.where(top, pltpu.roll(a, 4, 0), b))
    kept[...] = jnp.concatenate(inputs + cotangents, axis=0).astype(BF16)
    copies = [pltpu.make_async_copy(kept, out_ref.at[p], sems.at[p]) for p in range(out_ref.shape[0])]
    for copy in copies:
        copy.start()
    for copy in copies:
        copy.wait()


def forward(which_ref, plane_ref, gate_ref, up_ref, down_ref, out_ref):
    planes, rows, depth = plane_ref.shape
    half = rows // 2
    width = gate_ref.shape[1]
    inputs = plane_ref[:, :half, :].reshape(planes * half, depth)
    cotangents = plane_ref[:, half:, :].reshape(planes * half, depth)
    joined = jnp.concatenate([gate_ref[...], up_ref[...]], axis=1)
    out_ref[:, : 2 * width] = jnp.dot(inputs, joined, preferred_element_type=F32)
    out_ref[:, 2 * width :] = lax.dot_general(cotangents, down_ref[...], LAST, preferred_element_type=F32)


def run_forward(which, plane, gate_weight, up_weight, down_weight):
    planes, rows, depth = plane.shape
    width = gate_weight.shape[1]
    tokens = planes * rows // 4
    whole = lambda i, c: (0, 0)
    return call(
        forward,
        jax.ShapeDtypeStruct((tokens, 3 * width), F32),
        (6 * tokens * depth * width, plane.size + 6 * depth * width),
        grid_spec=pltpu.PrefetchScalarGridSpec(
            num_scalar_prefetch=1,
            grid=(1,),
            in_specs=[
                pl.BlockSpec((planes // 2, rows, depth), lambda i, c: (c[0], 0, 0)),
                pl.BlockSpec(gate_weight.shape, whole),
                pl.BlockSpec(up_weight.shape, whole),
                pl.BlockSpec(down_weight.shape, whole),
            ],
            out_specs=pl.BlockSpec((tokens, 3 * width), whole),
        ),
    )(which, plane, gate_weight, up_weight, down_weight)


def scale_pair(mine_ref, swapped_ref, out_ref):
    tokens = mine_ref.shape[0]
    pair = mine_ref[...] + swapped_ref[...]
    largest = jnp.max(jnp.abs(pair), axis=0, keepdims=True)
    power = jnp.floor(jnp.log2(jnp.maximum(largest, 1e-30)))
    out_ref[:tokens, :] = pair * jnp.exp2(-power) * 2.0**TOP
    out_ref[tokens:, :] = jnp.broadcast_to(power, (EXTRA, pair.shape[1]))


def activate(parts_ref, out_ref):
    tokens = out_ref.shape[0]
    width = out_ref.shape[1] // 3
    summed = 0.0
    for z in range(parts_ref.shape[0]):
        power = parts_ref[z, tokens:, :][:1]
        summed = summed + parts_ref[z, :tokens, :] * (jnp.exp2(power) * 2.0**-TOP)
    gate = summed[:, :width]
    up = summed[:, width : 2 * width]
    hidden_grad = summed[:, 2 * width :]
    sigma = 1.0 / (1.0 + jnp.exp(-gate))
    active = gate * sigma
    out_ref[:, :width] = (active * up).astype(BF16)
    out_ref[:, width : 2 * width] = (hidden_grad * up * sigma * (1.0 + gate * (1.0 - sigma))).astype(BF16)
    out_ref[:, 2 * width :] = (hidden_grad * active).astype(BF16)


def input_grads(triple_ref, gate_ref, up_ref, out_ref):
    tokens = triple_ref.shape[0]
    width = gate_ref.shape[1]
    depth = gate_ref.shape[0]
    both = triple_ref[:, width:]
    step = 256
    top = upper((tokens // 8, 8, step))
    for n in range(0, depth // 2, step):
        sides = []
        for at in (n, depth // 2 + n):
            joined = jnp.concatenate([gate_ref[at : at + step, :], up_ref[at : at + step, :]], axis=1)
            product = lax.dot_general(both, joined, LAST, preferred_element_type=F32)
            sides.append(product.reshape(tokens // 8, 8, step))
        left, right = sides
        out_ref[:, 0, :, n : n + step] = jnp.where(top, left, pltpu.roll(right, 4, 1)).astype(BF16)
        out_ref[:, 1, :, n : n + step] = jnp.where(top, pltpu.roll(left, 4, 1), right).astype(BF16)


def add_pieces(pieces_ref, out_ref):
    half = pieces_ref.shape[2]
    total = jnp.sum(pieces_ref[...].astype(F32), axis=0)
    out_ref[:, :half] = total[:4].astype(BF16)
    out_ref[:, half:] = pltpu.roll(total, 4, 0)[:4].astype(BF16)


def body(inputs, cotangent, gate_weight, up_weight, down_weight):
    own, depth = inputs.shape
    width = gate_weight.shape[1]
    columns = lax.axis_size("col")
    planes = lax.axis_size(DP)
    groups = columns * planes
    tokens = own * groups
    rows = 2 * columns * own
    shape = jax.ShapeDtypeStruct

    line = spread(jnp.concatenate([inputs, cotangent], axis=0), "col").reshape(columns, 2 * own, depth)
    copies = call(
        split_line,
        shape((planes, rows, depth), BF16),
        (0, planes * rows * depth * 2),
        limit=60,
        out_specs=pl.BlockSpec(memory_space=pltpu.HBM),
        scratch_shapes=[pltpu.VMEM((rows, depth), BF16), pltpu.SemaphoreType.DMA((planes,))],
    )(line)
    plane = exchange(copies, DP).reshape(planes, rows, depth)

    core = lax.axis_index("core").astype(jnp.int32).reshape(1)
    other = run_forward(1 - core, plane, gate_weight, up_weight, down_weight)
    swapped = lax.ppermute(other, "core", [(0, 1), (1, 0)])
    mine = run_forward(core, plane, gate_weight, up_weight, down_weight)
    scaled = call(
        scale_pair,
        shape((tokens // 2 + EXTRA, 3 * width), F32),
        (tokens * width * 10, tokens * width * 18),
    )(mine, swapped).astype(F16)
    scaled, later = lax.optimization_barrier((scaled, plane))
    parts = spread(scaled, "z_hi").reshape((lax.axis_size("z_hi"),) + scaled.shape)
    gathered_in = later[:, : rows // 2].reshape(tokens, depth)
    gathered_cot = later[:, rows // 2 :].reshape(tokens, depth)
    parts, gathered_in, gathered_cot = lax.optimization_barrier((parts, gathered_in, gathered_cot))

    triple = call(activate, shape((tokens // 2, 3 * width), BF16), (tokens * width * 10, parts.size * 4))(parts.astype(F32))
    triple = lax.all_gather(triple, "core", axis=0, tiled=True)

    partial_in = call(
        input_grads,
        shape((groups // 2, 2, 2 * own, depth // 2), BF16),
        (4 * tokens * depth * width, 2 * tokens * depth + 4 * depth * width),
    )(triple, gate_weight, up_weight)
    pieces = exchange(partial_in.reshape(groups, 2 * own, depth // 2), GROUP)
    grad_inputs = call(add_pieces, shape((own, depth), BF16), (tokens * depth, 2 * tokens * depth))(pieces)

    hidden, gate_grad, up_grad = (triple[:, i * width : (i + 1) * width] for i in range(3))
    product = functools.partial(lax.dot_general, dimension_numbers=FIRST, preferred_element_type=F32)
    grad_gate_weight = product(gathered_in, gate_grad).astype(BF16)
    grad_up_weight = product(gathered_in, up_grad).astype(BF16)
    grad_down_weight = product(hidden, gathered_cot).astype(BF16)
    return (grad_inputs, grad_gate_weight, grad_up_weight, grad_down_weight)


def solution(mesh):
    fine = Mesh(mesh.devices.reshape(2, 4, 4, 2, 8), ("z_lo", "x", "z_hi", "core", "col"))
    in_specs = (P(GROUP, ROW), P(GROUP, ROW), P(ROW, GROUP), P(ROW, GROUP), P(GROUP, ROW))
    out_specs = (P(GROUP, ROW), P(ROW, GROUP), P(ROW, GROUP), P(GROUP, ROW))
    return jax.shard_map(body, mesh=fine, in_specs=in_specs, out_specs=out_specs, check_vma=False)
```

```python
import jax
import jax.numpy as jnp
from jax import lax
from jax.experimental import pallas as pl
from jax.experimental.pallas import tpu as pltpu
from jax.sharding import Mesh
from jax.sharding import PartitionSpec as P

DP = ("z_lo", "x")
GROUP = ("z_lo", "x", "col")
ROW = ("z_hi", "core")
MIB = 1024 * 1024
EXTRA = 16
TOP = 14
F16 = jnp.float16
F32 = jnp.float32
BF16 = jnp.bfloat16
LAST = (((1,), (1,)), ((), ()))
FIRST = (((0,), (0,)), ((), ()))


def exchange(pieces, axes):
    return lax.all_to_all(pieces, axes, split_axis=0, concat_axis=0, tiled=True)


def spread(block, axes):
    n = lax.axis_size(axes)
    return exchange(jnp.broadcast_to(block[None], (n,) + block.shape), axes)


def call(kernel, out_shape, cost, limit=20, **rest):
    flops, size = cost
    return pl.pallas_call(
        kernel,
        out_shape=out_shape,
        cost_estimate=pl.CostEstimate(flops=flops, bytes_accessed=size, transcendentals=0),
        compiler_params=pltpu.CompilerParams(vmem_limit_bytes=limit * MIB),
        **rest,
    )


def upper(shape):
    return lax.broadcasted_iota(jnp.int32, shape, len(shape) - 2) < 4


def split_line(line_ref, out_ref, kept, sems):
    columns, _, depth = line_ref.shape
    blocks = line_ref[...].astype(F32)
    top = upper((8, depth))
    inputs, cotangents = [], []
    for j in range(columns // 2):
        a, b = blocks[2 * j], blocks[2 * j + 1]
        inputs.append(jnp.where(top, a, pltpu.roll(b, 4, 0)))
        cotangents.append(jnp.where(top, pltpu.roll(a, 4, 0), b))
    kept[...] = jnp.concatenate(inputs + cotangents, axis=0).astype(BF16)
    copies = [pltpu.make_async_copy(kept, out_ref.at[p], sems.at[p]) for p in range(out_ref.shape[0])]
    for copy in copies:
        copy.start()
    for copy in copies:
        copy.wait()


def forward(which_ref, plane_ref, gate_ref, up_ref, down_ref, out_ref):
    planes, rows, depth = plane_ref.shape
    half = rows // 2
    width = gate_ref.shape[1]
    inputs = plane_ref[:, :half, :].reshape(planes * half, depth)
    cotangents = plane_ref[:, half:, :].reshape(planes * half, depth)
    joined = jnp.concatenate([gate_ref[...], up_ref[...]], axis=1)
    out_ref[:, : 2 * width] = jnp.dot(inputs, joined, preferred_element_type=F32)
    out_ref[:, 2 * width :] = lax.dot_general(cotangents, down_ref[...], LAST, preferred_element_type=F32)


def run_forward(which, plane, gate_weight, up_weight, down_weight):
    planes, rows, depth = plane.shape
    width = gate_weight.shape[1]
    tokens = planes * rows // 4
    whole = lambda i, c: (0, 0)
    return call(
        forward,
        jax.ShapeDtypeStruct((tokens, 3 * width), F32),
        (6 * tokens * depth * width, plane.size + 6 * depth * width),
        grid_spec=pltpu.PrefetchScalarGridSpec(
            num_scalar_prefetch=1,
            grid=(1,),
            in_specs=[
                pl.BlockSpec((planes // 2, rows, depth), lambda i, c: (c[0], 0, 0)),
                pl.BlockSpec(gate_weight.shape, whole),
                pl.BlockSpec(up_weight.shape, whole),
                pl.BlockSpec(down_weight.shape, whole),
            ],
            out_specs=pl.BlockSpec((tokens, 3 * width), whole),
        ),
    )(which, plane, gate_weight, up_weight, down_weight)


def scale_pair(mine_ref, swapped_ref, out_ref):
    tokens = mine_ref.shape[0]
    pair = mine_ref[...] + swapped_ref[...]
    largest = jnp.max(jnp.abs(pair), axis=0, keepdims=True)
    power = jnp.floor(jnp.log2(jnp.maximum(largest, 1e-30)))
    out_ref[:tokens, :] = pair * jnp.exp2(-power) * 2.0**TOP
    out_ref[tokens:, :] = jnp.broadcast_to(power, (EXTRA, pair.shape[1]))


def activate(parts_ref, out_ref):
    tokens = out_ref.shape[0]
    width = out_ref.shape[1] // 3
    summed = 0.0
    for z in range(parts_ref.shape[0]):
        power = parts_ref[z, tokens:, :][:1]
        summed = summed + parts_ref[z, :tokens, :] * (jnp.exp2(power) * 2.0**-TOP)
    gate = summed[:, :width]
    up = summed[:, width : 2 * width]
    hidden_grad = summed[:, 2 * width :]
    sigma = 1.0 / (1.0 + jnp.exp(-gate))
    active = gate * sigma
    out_ref[:, :width] = (active * up).astype(BF16)
    out_ref[:, width : 2 * width] = (hidden_grad * up * sigma * (1.0 + gate * (1.0 - sigma))).astype(BF16)
    out_ref[:, 2 * width :] = (hidden_grad * active).astype(BF16)


def input_grads(triple_ref, gate_ref, up_ref, out_ref):
    tokens = triple_ref.shape[0]
    depth, width = gate_ref.shape
    both = triple_ref[:, width:]
    step = 256
    for n in range(0, depth, step):
        joined = jnp.concatenate([gate_ref[n : n + step, :], up_ref[n : n + step, :]], axis=1)
        product = lax.dot_general(both, joined, LAST, preferred_element_type=F32)
        out_ref[:, :, n : n + step] = product.reshape(out_ref.shape[:2] + (step,)).astype(BF16)


def add_planes(pieces_ref, out_ref):
    _, rows, depth = pieces_ref.shape
    half = depth // 2
    total = pieces_ref[0].astype(F32)
    for p in range(1, pieces_ref.shape[0]):
        total = total + pieces_ref[p].astype(F32)
    left = total[:, :half].reshape(rows // 8, 8, half)
    right = total[:, half:].reshape(rows // 8, 8, half)
    top = upper(left.shape)
    out_ref[:, 0] = jnp.where(top, left, pltpu.roll(right, 4, 1)).astype(BF16)
    out_ref[:, 1] = jnp.where(top, pltpu.roll(left, 4, 1), right).astype(BF16)


def weight_grads(triple_ref, plane_ref, gate_ref, up_ref, down_ref):
    planes, rows, step = plane_ref.shape
    half = rows // 2
    width = gate_ref.shape[1]
    inputs = plane_ref[:, :half, :].reshape(planes * half, step)
    cotangents = plane_ref[:, half:, :].reshape(planes * half, step)
    both = lax.dot_general(inputs, triple_ref[:, width:], FIRST, preferred_element_type=F32)
    gate_ref[...] = both[:, :width].astype(BF16)
    up_ref[...] = both[:, width:].astype(BF16)
    hidden = triple_ref[:, :width]
    down_ref[...] = lax.dot_general(hidden, cotangents, FIRST, preferred_element_type=F32).astype(BF16)


def add_pieces(pieces_ref, out_ref):
    half = pieces_ref.shape[2]
    total = jnp.sum(pieces_ref[...].astype(F32), axis=0)
    out_ref[:, :half] = total[:4].astype(BF16)
    out_ref[:, half:] = pltpu.roll(total, 4, 0)[:4].astype(BF16)


def body(inputs, cotangent, gate_weight, up_weight, down_weight):
    own, depth = inputs.shape
    width = gate_weight.shape[1]
    columns = lax.axis_size("col")
    planes = lax.axis_size(DP)
    groups = columns * planes
    tokens = own * groups
    rows = 2 * columns * own
    shape = jax.ShapeDtypeStruct

    line = spread(jnp.concatenate([inputs, cotangent], axis=0), "col").reshape(columns, 2 * own, depth)
    core = lax.axis_index("core").astype(jnp.int32).reshape(1)
    line, core, flipped = lax.optimization_barrier((line, core, 1 - core))
    copies = call(
        split_line,
        shape((planes, rows, depth), BF16),
        (0, planes * rows * depth * 2),
        out_specs=pl.BlockSpec(memory_space=pl.ANY),
        scratch_shapes=[pltpu.VMEM((rows, depth), BF16), pltpu.SemaphoreType.DMA((planes,))],
    )(line)
    plane = exchange(copies, DP).reshape(planes, rows, depth)

    other = run_forward(flipped, plane, gate_weight, up_weight, down_weight)
    swapped = lax.ppermute(other, "core", [(0, 1), (1, 0)])
    mine = run_forward(core, plane, gate_weight, up_weight, down_weight)
    scaled = call(
        scale_pair,
        shape((tokens // 2 + EXTRA, 3 * width), F32),
        (tokens * width * 10, tokens * width * 18),
    )(mine, swapped).astype(F16)
    parts = spread(scaled, "z_hi").reshape((lax.axis_size("z_hi"),) + scaled.shape)

    triple = call(activate, shape((tokens // 2, 3 * width), BF16), (tokens * width * 10, parts.size * 4))(parts.astype(F32))
    triple = lax.all_gather(triple, "core", axis=0, tiled=True)

    partial_in = call(
        input_grads,
        shape((planes, columns * own, depth), BF16),
        (4 * tokens * depth * width, 2 * tokens * depth + 4 * depth * width),
    )(triple, gate_weight, up_weight)
    line_in = call(
        add_planes,
        shape((columns // 2, 2, 2 * own, depth // 2), BF16),
        (tokens * depth, 2 * tokens * depth),
    )(exchange(partial_in, DP))
    line_in, later = lax.optimization_barrier((line_in, triple))
    pieces = exchange(line_in.reshape(columns, 2 * own, depth // 2), "col")
    step = depth // 4
    grad_gate_weight, grad_up_weight, grad_down_weight = call(
        weight_grads,
        [shape(w.shape, BF16) for w in (gate_weight, up_weight, down_weight)],
        (6 * tokens * depth * width, plane.size * 2 + 6 * depth * width),
        grid=(4,),
        in_specs=[
            pl.BlockSpec(triple.shape, lambda n: (0, 0)),
            pl.BlockSpec((planes, rows, step), lambda n: (0, 0, n)),
        ],
        out_specs=[
            pl.BlockSpec((step, width), lambda n: (n, 0)),
            pl.BlockSpec((step, width), lambda n: (n, 0)),
            pl.BlockSpec((width, step), lambda n: (0, n)),
        ],
    )(later, plane)
    grad_inputs = call(add_pieces, shape((own, depth), BF16), (columns * own * depth, 2 * columns * own * depth))(pieces)
    return (grad_inputs, grad_gate_weight, grad_up_weight, grad_down_weight)


def solution(mesh):
    fine = Mesh(mesh.devices.reshape(2, 4, 4, 2, 8), ("z_lo", "x", "z_hi", "core", "col"))
    in_specs = (P(GROUP, ROW), P(GROUP, ROW), P(ROW, GROUP), P(ROW, GROUP), P(GROUP, ROW))
    out_specs = (P(GROUP, ROW), P(ROW, GROUP), P(ROW, GROUP), P(GROUP, ROW))
    return jax.shard_map(body, mesh=fine, in_specs=in_specs, out_specs=out_specs, check_vma=False)
```

```python
import jax
import jax.numpy as jnp
from jax import lax
from jax.experimental import pallas as pl
from jax.experimental.pallas import tpu as pltpu
from jax.sharding import Mesh
from jax.sharding import PartitionSpec as P

DP = ("z_lo", "x")
GROUP = ("z_lo", "x", "col")
ROW = ("z_hi", "core")
MIB = 1024 * 1024
EXTRA = 8
TOP = 14
F16 = jnp.float16
F32 = jnp.float32
BF16 = jnp.bfloat16
LAST = (((1,), (1,)), ((), ()))
FIRST = (((0,), (0,)), ((), ()))


def exchange(pieces, axes):
    return lax.all_to_all(pieces, axes, split_axis=0, concat_axis=0, tiled=True)


def spread(block, axes):
    n = lax.axis_size(axes)
    return exchange(jnp.broadcast_to(block[None], (n,) + block.shape), axes)


def call(kernel, out_shape, cost, limit=20, **rest):
    flops, size = cost
    return pl.pallas_call(
        kernel,
        out_shape=out_shape,
        cost_estimate=pl.CostEstimate(flops=flops, bytes_accessed=size, transcendentals=0),
        compiler_params=pltpu.CompilerParams(vmem_limit_bytes=limit * MIB),
        **rest,
    )


def upper(shape):
    return lax.broadcasted_iota(jnp.int32, shape, len(shape) - 2) < 4


def split_line(line_ref, out_ref, kept, sems):
    columns, _, depth = line_ref.shape
    blocks = line_ref[...].astype(F32)
    top = upper((8, depth))
    inputs, cotangents = [], []
    for j in range(columns // 2):
        a, b = blocks[2 * j], blocks[2 * j + 1]
        inputs.append(jnp.where(top, a, pltpu.roll(b, 4, 0)))
        cotangents.append(jnp.where(top, pltpu.roll(a, 4, 0), b))
    kept[...] = jnp.concatenate(inputs + cotangents, axis=0).astype(BF16)
    copies = [pltpu.make_async_copy(kept, out_ref.at[p], sems.at[p]) for p in range(out_ref.shape[0])]
    for copy in copies:
        copy.start()
    for copy in copies:
        copy.wait()


def forward(plane_ref, gate_ref, up_ref, down_ref, out_ref):
    planes, rows, depth = plane_ref.shape
    half = rows // 2
    width = gate_ref.shape[1]
    inputs = plane_ref[:, :half, :].reshape(planes * half, depth)
    cotangents = plane_ref[:, half:, :].reshape(planes * half, depth)
    joined = jnp.concatenate([gate_ref[...], up_ref[...]], axis=1)
    out_ref[:, : 2 * width] = jnp.dot(inputs, joined, preferred_element_type=F32)
    out_ref[:, 2 * width :] = lax.dot_general(cotangents, down_ref[...], LAST, preferred_element_type=F32)


def scale_pair(core_ref, both_ref, out_ref):
    tokens = both_ref.shape[1]
    pair = both_ref[0] + both_ref[1]
    largest = jnp.max(jnp.abs(pair), axis=0, keepdims=True)
    power = jnp.floor(jnp.log2(jnp.maximum(largest, 1e-30)))
    out_ref[:tokens, :] = pair * jnp.exp2(-power) * 2.0**TOP
    out_ref[tokens:, :] = jnp.broadcast_to(power, (EXTRA, pair.shape[1]))


def activate(parts_ref, out_ref):
    tokens = out_ref.shape[0]
    width = out_ref.shape[1] // 3
    summed = 0.0
    for z in range(parts_ref.shape[0]):
        power = parts_ref[z, tokens:, :][:1]
        summed = summed + parts_ref[z, :tokens, :] * (jnp.exp2(power) * 2.0**-TOP)
    gate = summed[:, :width]
    up = summed[:, width : 2 * width]
    hidden_grad = summed[:, 2 * width :]
    sigma = 1.0 / (1.0 + jnp.exp(-gate))
    active = gate * sigma
    out_ref[:, :width] = (active * up).astype(BF16)
    out_ref[:, width : 2 * width] = (hidden_grad * up * sigma * (1.0 + gate * (1.0 - sigma))).astype(BF16)
    out_ref[:, 2 * width :] = (hidden_grad * active).astype(BF16)


def input_grads(triple_ref, gate_ref, up_ref, out_ref):
    tokens = triple_ref.shape[0]
    depth, width = gate_ref.shape
    both = triple_ref[:, width:]
    step = 256
    for n in range(0, depth, step):
        joined = jnp.concatenate([gate_ref[n : n + step, :], up_ref[n : n + step, :]], axis=1)
        product = lax.dot_general(both, joined, LAST, preferred_element_type=F32)
        out_ref[:, :, n : n + step] = product.reshape(out_ref.shape[:2] + (step,)).astype(BF16)


def add_planes(pieces_ref, out_ref):
    _, rows, depth = pieces_ref.shape
    half = depth // 2
    total = pieces_ref[0].astype(F32)
    for p in range(1, pieces_ref.shape[0]):
        total = total + pieces_ref[p].astype(F32)
    left = total[:, :half].reshape(rows // 8, 8, half)
    right = total[:, half:].reshape(rows // 8, 8, half)
    top = upper(left.shape)
    out_ref[:, 0] = jnp.where(top, left, pltpu.roll(right, 4, 1)).astype(BF16)
    out_ref[:, 1] = jnp.where(top, pltpu.roll(left, 4, 1), right).astype(BF16)


def weight_grads(triple_ref, plane_ref, gate_ref, up_ref, down_ref):
    planes, rows, step = plane_ref.shape
    half = rows // 2
    width = gate_ref.shape[1]
    inputs = plane_ref[:, :half, :].reshape(planes * half, step)
    cotangents = plane_ref[:, half:, :].reshape(planes * half, step)
    both = lax.dot_general(inputs, triple_ref[:, width:], FIRST, preferred_element_type=F32)
    gate_ref[...] = both[:, :width].astype(BF16)
    up_ref[...] = both[:, width:].astype(BF16)
    hidden = triple_ref[:, :width]
    down_ref[...] = lax.dot_general(hidden, cotangents, FIRST, preferred_element_type=F32).astype(BF16)


def add_pieces(pieces_ref, out_ref):
    half = pieces_ref.shape[2]
    total = jnp.sum(pieces_ref[...].astype(F32), axis=0)
    out_ref[:, :half] = total[:4].astype(BF16)
    out_ref[:, half:] = pltpu.roll(total, 4, 0)[:4].astype(BF16)


def body(inputs, cotangent, gate_weight, up_weight, down_weight):
    own, depth = inputs.shape
    width = gate_weight.shape[1]
    columns = lax.axis_size("col")
    planes = lax.axis_size(DP)
    groups = columns * planes
    tokens = own * groups
    rows = 2 * columns * own
    shape = jax.ShapeDtypeStruct

    block = jnp.concatenate([inputs, cotangent], axis=0)
    core = lax.axis_index("core").astype(jnp.int32).reshape(1)
    block, core = lax.optimization_barrier((block, core))
    line = spread(block, "col").reshape(columns, 2 * own, depth)
    copies = call(
        split_line,
        shape((planes, rows, depth), BF16),
        (0, planes * rows * depth * 2),
        out_specs=pl.BlockSpec(memory_space=pl.ANY),
        scratch_shapes=[pltpu.VMEM((rows, depth), BF16), pltpu.SemaphoreType.DMA((planes,))],
    )(line)
    plane = exchange(copies, DP).reshape(planes, rows, depth)

    partial = call(
        forward,
        shape((tokens, 3 * width), F32),
        (6 * tokens * depth * width, plane.size * 2 + 6 * depth * width),
    )(plane, gate_weight, up_weight, down_weight)
    both = lax.all_gather(partial, "core", axis=0, tiled=False)
    half = tokens // 2
    scaled = call(
        scale_pair,
        shape((half + EXTRA, 3 * width), F32),
        (tokens * width * 10, tokens * width * 18),
        grid_spec=pltpu.PrefetchScalarGridSpec(
            num_scalar_prefetch=1,
            grid=(1,),
            in_specs=[pl.BlockSpec((2, half, 3 * width), lambda i, c: (0, c[0], 0))],
            out_specs=pl.BlockSpec((half + EXTRA, 3 * width), lambda i, c: (0, 0)),
        ),
    )(core, both).astype(F16)
    parts = spread(scaled, "z_hi").reshape((lax.axis_size("z_hi"),) + scaled.shape)

    triple = call(activate, shape((tokens // 2, 3 * width), BF16), (tokens * width * 10, parts.size * 4))(parts.astype(F32))
    triple = lax.all_gather(triple, "core", axis=0, tiled=True)

    partial_in = call(
        input_grads,
        shape((planes, columns * own, depth), BF16),
        (4 * tokens * depth * width, 2 * tokens * depth + 4 * depth * width),
    )(triple, gate_weight, up_weight)
    line_in = call(
        add_planes,
        shape((columns // 2, 2, 2 * own, depth // 2), BF16),
        (tokens * depth, 2 * tokens * depth),
    )(exchange(partial_in, DP))
    line_in, later = lax.optimization_barrier((line_in, triple))
    pieces = exchange(line_in.reshape(columns, 2 * own, depth // 2), "col")
    step = depth // 4
    grad_gate_weight, grad_up_weight, grad_down_weight = call(
        weight_grads,
        [shape(w.shape, BF16) for w in (gate_weight, up_weight, down_weight)],
        (6 * tokens * depth * width, plane.size * 2 + 6 * depth * width),
        grid=(4,),
        in_specs=[
            pl.BlockSpec(triple.shape, lambda n: (0, 0)),
            pl.BlockSpec((planes, rows, step), lambda n: (0, 0, n)),
        ],
        out_specs=[
            pl.BlockSpec((step, width), lambda n: (n, 0)),
            pl.BlockSpec((step, width), lambda n: (n, 0)),
            pl.BlockSpec((width, step), lambda n: (0, n)),
        ],
    )(later, plane)
    grad_inputs = call(add_pieces, shape((own, depth), BF16), (columns * own * depth, 2 * columns * own * depth))(pieces)
    return (grad_inputs, grad_gate_weight, grad_up_weight, grad_down_weight)


def solution(mesh):
    fine = Mesh(mesh.devices.reshape(2, 4, 4, 2, 8), ("z_lo", "x", "z_hi", "core", "col"))
    in_specs = (P(GROUP, ROW), P(GROUP, ROW), P(ROW, GROUP), P(ROW, GROUP), P(GROUP, ROW))
    out_specs = (P(GROUP, ROW), P(ROW, GROUP), P(ROW, GROUP), P(GROUP, ROW))
    return jax.shard_map(body, mesh=fine, in_specs=in_specs, out_specs=out_specs, check_vma=False)
```

```python
import jax
import jax.numpy as jnp
from jax import lax
from jax.experimental import pallas as pl
from jax.experimental.pallas import tpu as pltpu
from jax.sharding import Mesh
from jax.sharding import PartitionSpec as P

SLAB = ("z_lo", "col")
PLANES = ("x", "z_lo")
GROUP = ("z_lo", "x", "col")
ROW = ("z_hi", "core")
MIB = 1024 * 1024
EXTRA = 8
TOP = 14
F16 = jnp.float16
F32 = jnp.float32
BF16 = jnp.bfloat16
LAST = (((1,), (1,)), ((), ()))
FIRST = (((0,), (0,)), ((), ()))


def exchange(pieces, axes):
    return lax.all_to_all(pieces, axes, split_axis=0, concat_axis=0, tiled=True)


def spread(block, axes):
    n = lax.axis_size(axes)
    return exchange(jnp.broadcast_to(block[None], (n,) + block.shape), axes)


def call(kernel, out_shape, cost, limit=20, **rest):
    flops, size = cost
    return pl.pallas_call(
        kernel,
        out_shape=out_shape,
        cost_estimate=pl.CostEstimate(flops=flops, bytes_accessed=size, transcendentals=0),
        compiler_params=pltpu.CompilerParams(vmem_limit_bytes=limit * MIB),
        **rest,
    )


def upper(shape):
    return lax.broadcasted_iota(jnp.int32, shape, len(shape) - 2) < 4


def split_line(line_ref, out_ref, kept, sems):
    count, _, depth = line_ref.shape
    blocks = line_ref[...].astype(F32)
    top = upper((8, depth))
    inputs, cotangents = [], []
    for j in range(count // 2):
        a, b = blocks[2 * j], blocks[2 * j + 1]
        inputs.append(jnp.where(top, a, pltpu.roll(b, 4, 0)))
        cotangents.append(jnp.where(top, pltpu.roll(a, 4, 0), b))
    kept[...] = jnp.concatenate(inputs + cotangents, axis=0).astype(BF16)
    copies = [pltpu.make_async_copy(kept, out_ref.at[p], sems.at[p]) for p in range(out_ref.shape[0])]
    for copy in copies:
        copy.start()
    for copy in copies:
        copy.wait()


def forward(plane_ref, gate_ref, up_ref, down_ref, out_ref):
    planes, rows, depth = plane_ref.shape
    half = rows // 2
    width = gate_ref.shape[1]
    inputs = plane_ref[:, :half, :].reshape(planes * half, depth)
    cotangents = plane_ref[:, half:, :].reshape(planes * half, depth)
    joined = jnp.concatenate([gate_ref[...], up_ref[...]], axis=1)
    out_ref[:, : 2 * width] = jnp.dot(inputs, joined, preferred_element_type=F32)
    out_ref[:, 2 * width :] = lax.dot_general(cotangents, down_ref[...], LAST, preferred_element_type=F32)


def scale_pair(core_ref, both_ref, out_ref):
    tokens = both_ref.shape[1]
    pair = both_ref[0] + both_ref[1]
    largest = jnp.max(jnp.abs(pair), axis=0, keepdims=True)
    power = jnp.floor(jnp.log2(jnp.maximum(largest, 1e-30)))
    out_ref[:tokens, :] = pair * jnp.exp2(-power) * 2.0**TOP
    out_ref[tokens:, :] = jnp.broadcast_to(power, (EXTRA, pair.shape[1]))


def activate(parts_ref, out_ref):
    tokens = out_ref.shape[0]
    width = out_ref.shape[1] // 3
    summed = 0.0
    for z in range(parts_ref.shape[0]):
        power = parts_ref[z, tokens:, :][:1]
        summed = summed + parts_ref[z, :tokens, :] * (jnp.exp2(power) * 2.0**-TOP)
    gate = summed[:, :width]
    up = summed[:, width : 2 * width]
    hidden_grad = summed[:, 2 * width :]
    sigma = 1.0 / (1.0 + jnp.exp(-gate))
    active = gate * sigma
    out_ref[:, :width] = (active * up).astype(BF16)
    out_ref[:, width : 2 * width] = (hidden_grad * up * sigma * (1.0 + gate * (1.0 - sigma))).astype(BF16)
    out_ref[:, 2 * width :] = (hidden_grad * active).astype(BF16)


def input_grads(triple_ref, gate_ref, up_ref, out_ref):
    tokens = triple_ref.shape[0]
    depth, width = gate_ref.shape
    both = triple_ref[:, width:]
    step = 256
    for n in range(0, depth, step):
        joined = jnp.concatenate([gate_ref[n : n + step, :], up_ref[n : n + step, :]], axis=1)
        product = lax.dot_general(both, joined, LAST, preferred_element_type=F32)
        out_ref[:, :, n : n + step] = product.reshape(out_ref.shape[:2] + (step,)).astype(BF16)


def add_planes(pieces_ref, out_ref):
    _, rows, depth = pieces_ref.shape
    half = depth // 2
    total = pieces_ref[0].astype(F32)
    for p in range(1, pieces_ref.shape[0]):
        total = total + pieces_ref[p].astype(F32)
    left = total[:, :half].reshape(rows // 8, 8, half)
    right = total[:, half:].reshape(rows // 8, 8, half)
    top = upper(left.shape)
    out_ref[:, 0] = jnp.where(top, left, pltpu.roll(right, 4, 1)).astype(BF16)
    out_ref[:, 1] = jnp.where(top, pltpu.roll(left, 4, 1), right).astype(BF16)


def weight_grads(triple_ref, plane_ref, gate_ref, up_ref, down_ref):
    planes, rows, step = plane_ref.shape
    half = rows // 2
    width = gate_ref.shape[1]
    inputs = plane_ref[:, :half, :].reshape(planes * half, step)
    cotangents = plane_ref[:, half:, :].reshape(planes * half, step)
    both = lax.dot_general(inputs, triple_ref[:, width:], FIRST, preferred_element_type=F32)
    gate_ref[...] = both[:, :width].astype(BF16)
    up_ref[...] = both[:, width:].astype(BF16)
    hidden = triple_ref[:, :width]
    down_ref[...] = lax.dot_general(hidden, cotangents, FIRST, preferred_element_type=F32).astype(BF16)


def add_pieces(pieces_ref, out_ref):
    half = pieces_ref.shape[2]
    total = jnp.sum(pieces_ref[...].astype(F32), axis=0)
    out_ref[:, :half] = total[:4].astype(BF16)
    out_ref[:, half:] = pltpu.roll(total, 4, 0)[:4].astype(BF16)


def body(inputs, cotangent, gate_weight, up_weight, down_weight):
    own, depth = inputs.shape
    width = gate_weight.shape[1]
    columns = lax.axis_size("col")
    planes = lax.axis_size(PLANES)
    slabs = lax.axis_size("x")
    groups = columns * planes
    tokens = own * groups
    rows = 2 * tokens // slabs
    shape = jax.ShapeDtypeStruct

    block = jnp.concatenate([inputs, cotangent], axis=0)
    core = lax.axis_index("core").astype(jnp.int32).reshape(1)
    block, core = lax.optimization_barrier((block, core))
    line = spread(block, SLAB).reshape(groups // slabs, 2 * own, depth)
    copies = call(
        split_line,
        shape((slabs, rows, depth), BF16),
        (0, slabs * rows * depth * 2),
        out_specs=pl.BlockSpec(memory_space=pl.ANY),
        scratch_shapes=[pltpu.VMEM((rows, depth), BF16), pltpu.SemaphoreType.DMA((slabs,))],
    )(line)
    plane = exchange(copies, "x").reshape(slabs, rows, depth)

    partial = call(
        forward,
        shape((tokens, 3 * width), F32),
        (6 * tokens * depth * width, plane.size * 2 + 6 * depth * width),
    )(plane, gate_weight, up_weight, down_weight)
    both = lax.all_gather(partial, "core", axis=0, tiled=False)
    half = tokens // 2
    scaled = call(
        scale_pair,
        shape((half + EXTRA, 3 * width), F32),
        (tokens * width * 10, tokens * width * 18),
        grid_spec=pltpu.PrefetchScalarGridSpec(
            num_scalar_prefetch=1,
            grid=(1,),
            in_specs=[pl.BlockSpec((2, half, 3 * width), lambda i, c: (0, c[0], 0))],
            out_specs=pl.BlockSpec((half + EXTRA, 3 * width), lambda i, c: (0, 0)),
        ),
    )(core, both).astype(F16)
    parts = spread(scaled, "z_hi").reshape((lax.axis_size("z_hi"),) + scaled.shape)

    triple = call(activate, shape((tokens // 2, 3 * width), BF16), (tokens * width * 10, parts.size * 4))(parts.astype(F32))
    triple = lax.all_gather(triple, "core", axis=0, tiled=True)

    partial_in = call(
        input_grads,
        shape((planes, columns * own, depth), BF16),
        (4 * tokens * depth * width, 2 * tokens * depth + 4 * depth * width),
    )(triple, gate_weight, up_weight)
    line_in = call(
        add_planes,
        shape((columns // 2, 2, 2 * own, depth // 2), BF16),
        (tokens * depth, 2 * tokens * depth),
    )(exchange(partial_in, PLANES))
    line_in, later = lax.optimization_barrier((line_in, triple))
    pieces = exchange(line_in.reshape(columns, 2 * own, depth // 2), "col")
    step = depth // 4
    grad_gate_weight, grad_up_weight, grad_down_weight = call(
        weight_grads,
        [shape(w.shape, BF16) for w in (gate_weight, up_weight, down_weight)],
        (6 * tokens * depth * width, plane.size * 2 + 6 * depth * width),
        grid=(4,),
        in_specs=[
            pl.BlockSpec(triple.shape, lambda n: (0, 0)),
            pl.BlockSpec((slabs, rows, step), lambda n: (0, 0, n)),
        ],
        out_specs=[
            pl.BlockSpec((step, width), lambda n: (n, 0)),
            pl.BlockSpec((step, width), lambda n: (n, 0)),
            pl.BlockSpec((width, step), lambda n: (0, n)),
        ],
    )(later, plane)
    grad_inputs = call(add_pieces, shape((own, depth), BF16), (columns * own * depth, 2 * columns * own * depth))(pieces)
    return (grad_inputs, grad_gate_weight, grad_up_weight, grad_down_weight)


def solution(mesh):
    fine = Mesh(mesh.devices.reshape(2, 4, 4, 2, 8), ("z_lo", "x", "z_hi", "core", "col"))
    in_specs = (P(GROUP, ROW), P(GROUP, ROW), P(ROW, GROUP), P(ROW, GROUP), P(GROUP, ROW))
    out_specs = (P(GROUP, ROW), P(ROW, GROUP), P(ROW, GROUP), P(GROUP, ROW))
    return jax.shard_map(body, mesh=fine, in_specs=in_specs, out_specs=out_specs, check_vma=False)
```

```python
import jax
import jax.numpy as jnp
from jax import lax
from jax.experimental import pallas as pl
from jax.experimental.pallas import tpu as pltpu
from jax.sharding import Mesh
from jax.sharding import PartitionSpec as P

DP = ("z_lo", "x")
GROUP = ("z_lo", "x", "col")
ROW = ("z_hi", "core")
FIRST_PAIRS = ((0, 1), (2, 3))
SECOND_PAIRS = ((0, 3), (1, 2))
MIB = 1024 * 1024
EXTRA = 8
TOP = 14
F16 = jnp.float16
F32 = jnp.float32
BF16 = jnp.bfloat16
LAST = (((1,), (1,)), ((), ()))
FIRST = (((0,), (0,)), ((), ()))


def exchange(pieces, axes):
    return lax.all_to_all(pieces, axes, split_axis=0, concat_axis=0, tiled=True)


def spread(block, axes):
    n = lax.axis_size(axes)
    return exchange(jnp.broadcast_to(block[None], (n,) + block.shape), axes)


def call(kernel, out_shape, cost, limit=20, **rest):
    flops, size = cost
    return pl.pallas_call(
        kernel,
        out_shape=out_shape,
        cost_estimate=pl.CostEstimate(flops=flops, bytes_accessed=size, transcendentals=0),
        compiler_params=pltpu.CompilerParams(vmem_limit_bytes=limit * MIB),
        **rest,
    )


def upper(shape):
    return lax.broadcasted_iota(jnp.int32, shape, len(shape) - 2) < 4


def split_line(line_ref, out_ref, kept, sems):
    columns, _, depth = line_ref.shape
    blocks = line_ref[...].astype(F32)
    top = upper((8, depth))
    inputs, cotangents = [], []
    for j in range(columns // 2):
        a, b = blocks[2 * j], blocks[2 * j + 1]
        inputs.append(jnp.where(top, a, pltpu.roll(b, 4, 0)))
        cotangents.append(jnp.where(top, pltpu.roll(a, 4, 0), b))
    kept[...] = jnp.concatenate(inputs + cotangents, axis=0).astype(BF16)
    copies = [pltpu.make_async_copy(kept, out_ref.at[p], sems.at[p]) for p in range(out_ref.shape[0])]
    for copy in copies:
        copy.start()
    for copy in copies:
        copy.wait()


def forward(plane_ref, gate_ref, up_ref, down_ref, out_ref):
    planes, rows, depth = plane_ref.shape
    half = rows // 2
    width = gate_ref.shape[1]
    inputs = plane_ref[:, :half, :].reshape(planes * half, depth)
    cotangents = plane_ref[:, half:, :].reshape(planes * half, depth)
    joined = jnp.concatenate([gate_ref[...], up_ref[...]], axis=1)
    out_ref[:, : 2 * width] = jnp.dot(inputs, joined, preferred_element_type=F32)
    out_ref[:, 2 * width :] = lax.dot_general(cotangents, down_ref[...], LAST, preferred_element_type=F32)


def store_scaled(pair, out_ref):
    tokens = pair.shape[0]
    largest = jnp.max(jnp.abs(pair), axis=0, keepdims=True)
    power = jnp.floor(jnp.log2(jnp.maximum(largest, 1e-30)))
    out_ref[:tokens, :] = pair * jnp.exp2(-power) * 2.0**TOP
    out_ref[tokens:, :] = jnp.broadcast_to(power, (EXTRA, pair.shape[1]))


def sum_scaled(parts_ref):
    tokens = parts_ref.shape[1] - EXTRA
    summed = 0.0
    for z in range(parts_ref.shape[0]):
        power = parts_ref[z, tokens:, :][:1]
        summed = summed + parts_ref[z, :tokens, :] * (jnp.exp2(power) * 2.0**-TOP)
    return summed


def scale_pair(core_ref, both_ref, out_ref):
    store_scaled(both_ref[0] + both_ref[1], out_ref)


def rescale(parts_ref, out_ref):
    store_scaled(sum_scaled(parts_ref), out_ref)


def activate(parts_ref, out_ref):
    width = out_ref.shape[1] // 3
    summed = sum_scaled(parts_ref)
    gate = summed[:, :width]
    up = summed[:, width : 2 * width]
    hidden_grad = summed[:, 2 * width :]
    sigma = 1.0 / (1.0 + jnp.exp(-gate))
    active = gate * sigma
    out_ref[:, :width] = (active * up).astype(BF16)
    out_ref[:, width : 2 * width] = (hidden_grad * up * sigma * (1.0 + gate * (1.0 - sigma))).astype(BF16)
    out_ref[:, 2 * width :] = (hidden_grad * active).astype(BF16)


def input_grads(triple_ref, gate_ref, up_ref, out_ref):
    tokens = triple_ref.shape[0]
    depth, width = gate_ref.shape
    both = triple_ref[:, width:]
    step = 256
    for n in range(0, depth, step):
        joined = jnp.concatenate([gate_ref[n : n + step, :], up_ref[n : n + step, :]], axis=1)
        product = lax.dot_general(both, joined, LAST, preferred_element_type=F32)
        out_ref[:, :, n : n + step] = product.reshape(out_ref.shape[:2] + (step,)).astype(BF16)


def add_planes(pieces_ref, out_ref):
    _, rows, depth = pieces_ref.shape
    half = depth // 2
    total = pieces_ref[0].astype(F32)
    for p in range(1, pieces_ref.shape[0]):
        total = total + pieces_ref[p].astype(F32)
    left = total[:, :half].reshape(rows // 8, 8, half)
    right = total[:, half:].reshape(rows // 8, 8, half)
    top = upper(left.shape)
    out_ref[:, 0] = jnp.where(top, left, pltpu.roll(right, 4, 1)).astype(BF16)
    out_ref[:, 1] = jnp.where(top, pltpu.roll(left, 4, 1), right).astype(BF16)


def weight_grads(triple_ref, plane_ref, gate_ref, up_ref, down_ref):
    planes, rows, step = plane_ref.shape
    half = rows // 2
    width = gate_ref.shape[1]
    inputs = plane_ref[:, :half, :].reshape(planes * half, step)
    cotangents = plane_ref[:, half:, :].reshape(planes * half, step)
    both = lax.dot_general(inputs, triple_ref[:, width:], FIRST, preferred_element_type=F32)
    gate_ref[...] = both[:, :width].astype(BF16)
    up_ref[...] = both[:, width:].astype(BF16)
    hidden = triple_ref[:, :width]
    down_ref[...] = lax.dot_general(hidden, cotangents, FIRST, preferred_element_type=F32).astype(BF16)


def add_pieces(pieces_ref, out_ref):
    half = pieces_ref.shape[2]
    total = jnp.sum(pieces_ref[...].astype(F32), axis=0)
    out_ref[:, :half] = total[:4].astype(BF16)
    out_ref[:, half:] = pltpu.roll(total, 4, 0)[:4].astype(BF16)


def body(inputs, cotangent, gate_weight, up_weight, down_weight):
    own, depth = inputs.shape
    width = gate_weight.shape[1]
    columns = lax.axis_size("col")
    planes = lax.axis_size(DP)
    groups = columns * planes
    tokens = own * groups
    rows = 2 * columns * own
    shape = jax.ShapeDtypeStruct

    block = jnp.concatenate([inputs, cotangent], axis=0)
    core = lax.axis_index("core").astype(jnp.int32).reshape(1)
    block, core = lax.optimization_barrier((block, core))
    line = spread(block, "col").reshape(columns, 2 * own, depth)
    copies = call(
        split_line,
        shape((planes, rows, depth), BF16),
        (0, planes * rows * depth * 2),
        out_specs=pl.BlockSpec(memory_space=pl.ANY),
        scratch_shapes=[pltpu.VMEM((rows, depth), BF16), pltpu.SemaphoreType.DMA((planes,))],
    )(line)
    plane = exchange(copies, DP).reshape(planes, rows, depth)

    partial = call(
        forward,
        shape((tokens, 3 * width), F32),
        (6 * tokens * depth * width, plane.size * 2 + 6 * depth * width),
    )(plane, gate_weight, up_weight, down_weight)
    both = lax.all_gather(partial, "core", axis=0, tiled=False)
    half = tokens // 2
    scaled = call(
        scale_pair,
        shape((half + EXTRA, 3 * width), F32),
        (tokens * width * 10, tokens * width * 18),
        grid_spec=pltpu.PrefetchScalarGridSpec(
            num_scalar_prefetch=1,
            grid=(1,),
            in_specs=[pl.BlockSpec((2, half, 3 * width), lambda i, c: (0, c[0], 0))],
            out_specs=pl.BlockSpec((half + EXTRA, 3 * width), lambda i, c: (0, 0)),
        ),
    )(core, both).astype(F16)
    parts = lax.all_gather(scaled, "z_hi", axis=0, tiled=False, axis_index_groups=FIRST_PAIRS)
    scaled = call(rescale, shape(scaled.shape, F32), (tokens * width * 10, parts.size * 4))(parts.astype(F32)).astype(F16)
    parts = lax.all_gather(scaled, "z_hi", axis=0, tiled=False, axis_index_groups=SECOND_PAIRS)

    triple = call(activate, shape((tokens // 2, 3 * width), BF16), (tokens * width * 10, parts.size * 4))(parts.astype(F32))
    triple = lax.all_gather(triple, "core", axis=0, tiled=True)

    partial_in = call(
        input_grads,
        shape((planes, columns * own, depth), BF16),
        (4 * tokens * depth * width, 2 * tokens * depth + 4 * depth * width),
    )(triple, gate_weight, up_weight)
    line_in = call(
        add_planes,
        shape((columns // 2, 2, 2 * own, depth // 2), BF16),
        (tokens * depth, 2 * tokens * depth),
    )(exchange(partial_in, DP))
    line_in, later = lax.optimization_barrier((line_in, triple))
    pieces = exchange(line_in.reshape(columns, 2 * own, depth // 2), "col")
    step = depth // 4
    grad_gate_weight, grad_up_weight, grad_down_weight = call(
        weight_grads,
        [shape(w.shape, BF16) for w in (gate_weight, up_weight, down_weight)],
        (6 * tokens * depth * width, plane.size * 2 + 6 * depth * width),
        grid=(4,),
        in_specs=[
            pl.BlockSpec(triple.shape, lambda n: (0, 0)),
            pl.BlockSpec((planes, rows, step), lambda n: (0, 0, n)),
        ],
        out_specs=[
            pl.BlockSpec((step, width), lambda n: (n, 0)),
            pl.BlockSpec((step, width), lambda n: (n, 0)),
            pl.BlockSpec((width, step), lambda n: (0, n)),
        ],
    )(later, plane)
    grad_inputs = call(add_pieces, shape((own, depth), BF16), (columns * own * depth, 2 * columns * own * depth))(pieces)
    return (grad_inputs, grad_gate_weight, grad_up_weight, grad_down_weight)


def solution(mesh):
    fine = Mesh(mesh.devices.reshape(2, 4, 4, 2, 8), ("z_lo", "x", "z_hi", "core", "col"))
    in_specs = (P(GROUP, ROW), P(GROUP, ROW), P(ROW, GROUP), P(ROW, GROUP), P(GROUP, ROW))
    out_specs = (P(GROUP, ROW), P(ROW, GROUP), P(ROW, GROUP), P(GROUP, ROW))
    return jax.shard_map(body, mesh=fine, in_specs=in_specs, out_specs=out_specs, check_vma=False)
```

```python
import jax
import jax.numpy as jnp
from jax import lax
from jax.experimental import pallas as pl
from jax.experimental.pallas import tpu as pltpu
from jax.sharding import Mesh
from jax.sharding import PartitionSpec as P

DP = ("z_lo", "x")
NEAR = ("z_lo", "x", "y_lo")
COLUMN = ("y_lo", "y_hi")
GROUP = ("z_lo", "x", "y_hi", "y_lo")
ROW = ("z_hi", "core")
FIRST_PAIRS = ((0, 1), (2, 3))
SECOND_PAIRS = ((0, 3), (1, 2))
MIB = 1024 * 1024
EXTRA = 8
TOP = 14
F16 = jnp.float16
F32 = jnp.float32
BF16 = jnp.bfloat16
LAST = (((1,), (1,)), ((), ()))
FIRST = (((0,), (0,)), ((), ()))


def exchange(pieces, axes):
    return lax.all_to_all(pieces, axes, split_axis=0, concat_axis=0, tiled=True)


def spread(block, axes):
    n = lax.axis_size(axes)
    return exchange(jnp.broadcast_to(block[None], (n,) + block.shape), axes)


def call(kernel, out_shape, cost, limit=20, **rest):
    flops, size = cost
    return pl.pallas_call(
        kernel,
        out_shape=out_shape,
        cost_estimate=pl.CostEstimate(flops=flops, bytes_accessed=size, transcendentals=0),
        compiler_params=pltpu.CompilerParams(vmem_limit_bytes=limit * MIB),
        **rest,
    )


def upper(shape):
    return lax.broadcasted_iota(jnp.int32, shape, len(shape) - 2) < 4


def split_line(line_ref, out_ref):
    columns, _, depth = line_ref.shape
    blocks = line_ref[...].astype(F32)
    top = upper((8, depth))
    inputs, cotangents = [], []
    for j in range(columns // 2):
        a, b = blocks[2 * j], blocks[2 * j + 1]
        inputs.append(jnp.where(top, a, pltpu.roll(b, 4, 0)))
        cotangents.append(jnp.where(top, pltpu.roll(a, 4, 0), b))
    rows = jnp.concatenate(inputs + cotangents, axis=0).astype(BF16)
    for p in range(out_ref.shape[0]):
        out_ref[p] = rows


def forward(plane_ref, gate_ref, up_ref, down_ref, out_ref):
    planes, rows, depth = plane_ref.shape
    half = rows // 2
    width = gate_ref.shape[1]
    inputs = plane_ref[:, :half, :].reshape(planes * half, depth)
    cotangents = plane_ref[:, half:, :].reshape(planes * half, depth)
    joined = jnp.concatenate([gate_ref[...], up_ref[...]], axis=1)
    out_ref[:, : 2 * width] = jnp.dot(inputs, joined, preferred_element_type=F32)
    out_ref[:, 2 * width :] = lax.dot_general(cotangents, down_ref[...], LAST, preferred_element_type=F32)


def store_scaled(pair, out_ref):
    tokens = pair.shape[0]
    largest = jnp.max(jnp.abs(pair), axis=0, keepdims=True)
    power = jnp.floor(jnp.log2(jnp.maximum(largest, 1e-30)))
    out_ref[:tokens, :] = pair * jnp.exp2(-power) * 2.0**TOP
    out_ref[tokens:, :] = jnp.broadcast_to(power, (EXTRA, pair.shape[1]))


def sum_scaled(parts_ref):
    tokens = parts_ref.shape[1] - EXTRA
    summed = 0.0
    for z in range(parts_ref.shape[0]):
        power = parts_ref[z, tokens:, :][:1]
        summed = summed + parts_ref[z, :tokens, :] * (jnp.exp2(power) * 2.0**-TOP)
    return summed


def scale_pair(core_ref, both_ref, out_ref):
    store_scaled(both_ref[0] + both_ref[1], out_ref)


def rescale(parts_ref, out_ref):
    store_scaled(sum_scaled(parts_ref), out_ref)


def activate(parts_ref, out_ref):
    width = out_ref.shape[1] // 3
    summed = sum_scaled(parts_ref)
    gate = summed[:, :width]
    up = summed[:, width : 2 * width]
    hidden_grad = summed[:, 2 * width :]
    sigma = 1.0 / (1.0 + jnp.exp(-gate))
    active = gate * sigma
    out_ref[:, :width] = (active * up).astype(BF16)
    out_ref[:, width : 2 * width] = (hidden_grad * up * sigma * (1.0 + gate * (1.0 - sigma))).astype(BF16)
    out_ref[:, 2 * width :] = (hidden_grad * active).astype(BF16)


def input_grads(triple_ref, gate_ref, up_ref, out_ref):
    tokens = triple_ref.shape[0]
    depth, width = gate_ref.shape
    both = triple_ref[:, width:]
    step = 256
    for n in range(0, depth, step):
        joined = jnp.concatenate([gate_ref[n : n + step, :], up_ref[n : n + step, :]], axis=1)
        product = lax.dot_general(both, joined, LAST, preferred_element_type=F32)
        out_ref[:, :, n : n + step] = product.reshape(out_ref.shape[:2] + (step,)).astype(BF16)


def add_planes(pieces_ref, out_ref):
    _, rows, depth = pieces_ref.shape
    half = depth // 2
    total = pieces_ref[0].astype(F32)
    for p in range(1, pieces_ref.shape[0]):
        total = total + pieces_ref[p].astype(F32)
    left = total[:, :half].reshape(rows // 8, 8, half)
    right = total[:, half:].reshape(rows // 8, 8, half)
    top = upper(left.shape)
    out_ref[:, 0] = jnp.where(top, left, pltpu.roll(right, 4, 1)).astype(BF16)
    out_ref[:, 1] = jnp.where(top, pltpu.roll(left, 4, 1), right).astype(BF16)


def weight_grads(triple_ref, plane_ref, gate_ref, up_ref, down_ref):
    planes, rows, step = plane_ref.shape
    half = rows // 2
    width = gate_ref.shape[1]
    inputs = plane_ref[:, :half, :].reshape(planes * half, step)
    cotangents = plane_ref[:, half:, :].reshape(planes * half, step)
    both = lax.dot_general(inputs, triple_ref[:, width:], FIRST, preferred_element_type=F32)
    gate_ref[...] = both[:, :width].astype(BF16)
    up_ref[...] = both[:, width:].astype(BF16)
    hidden = triple_ref[:, :width]
    down_ref[...] = lax.dot_general(hidden, cotangents, FIRST, preferred_element_type=F32).astype(BF16)


def add_pieces(pieces_ref, out_ref):
    half = pieces_ref.shape[2]
    total = jnp.sum(pieces_ref[...].astype(F32), axis=0)
    out_ref[:, :half] = total[:4].astype(BF16)
    out_ref[:, half:] = pltpu.roll(total, 4, 0)[:4].astype(BF16)


def body(inputs, cotangent, gate_weight, up_weight, down_weight):
    own, depth = inputs.shape
    width = gate_weight.shape[1]
    columns = lax.axis_size(COLUMN)
    planes = lax.axis_size(DP)
    groups = columns * planes
    tokens = own * groups
    near = lax.axis_size(NEAR)
    rows = 2 * tokens // near
    shape = jax.ShapeDtypeStruct

    block = jnp.concatenate([inputs, cotangent], axis=0)
    core = lax.axis_index("core").astype(jnp.int32).reshape(1)
    block, core = lax.optimization_barrier((block, core))
    line = spread(block, "y_hi").reshape(groups // near, 2 * own, depth)
    copies = call(
        split_line,
        shape((near, rows, depth), BF16),
        (0, near * rows * depth * 2),
    )(line)
    plane = exchange(copies, NEAR).reshape(near, rows, depth)

    partial = call(
        forward,
        shape((tokens, 3 * width), F32),
        (6 * tokens * depth * width, plane.size * 2 + 6 * depth * width),
    )(plane, gate_weight, up_weight, down_weight)
    both = lax.all_gather(partial, "core", axis=0, tiled=False)
    half = tokens // 2
    scaled = call(
        scale_pair,
        shape((half + EXTRA, 3 * width), F32),
        (tokens * width * 10, tokens * width * 18),
        grid_spec=pltpu.PrefetchScalarGridSpec(
            num_scalar_prefetch=1,
            grid=(1,),
            in_specs=[pl.BlockSpec((2, half, 3 * width), lambda i, c: (0, c[0], 0))],
            out_specs=pl.BlockSpec((half + EXTRA, 3 * width), lambda i, c: (0, 0)),
        ),
    )(core, both).astype(F16)
    parts = lax.all_gather(scaled, "z_hi", axis=0, tiled=False, axis_index_groups=FIRST_PAIRS)
    scaled = call(rescale, shape(scaled.shape, F32), (tokens * width * 10, parts.size * 4))(parts.astype(F32)).astype(F16)
    parts = lax.all_gather(scaled, "z_hi", axis=0, tiled=False, axis_index_groups=SECOND_PAIRS)

    triple = call(activate, shape((tokens // 2, 3 * width), BF16), (tokens * width * 10, parts.size * 4))(parts.astype(F32))
    triple = lax.all_gather(triple, "core", axis=0, tiled=True)

    partial_in = call(
        input_grads,
        shape((planes, columns * own, depth), BF16),
        (4 * tokens * depth * width, 2 * tokens * depth + 4 * depth * width),
    )(triple, gate_weight, up_weight)
    line_in = call(
        add_planes,
        shape((columns // 2, 2, 2 * own, depth // 2), BF16),
        (tokens * depth, 2 * tokens * depth),
    )(exchange(partial_in, DP))
    line_in, later = lax.optimization_barrier((line_in, triple))
    pieces = exchange(line_in.reshape(columns, 2 * own, depth // 2), COLUMN)
    step = depth // 4
    grad_gate_weight, grad_up_weight, grad_down_weight = call(
        weight_grads,
        [shape(w.shape, BF16) for w in (gate_weight, up_weight, down_weight)],
        (6 * tokens * depth * width, plane.size * 2 + 6 * depth * width),
        grid=(4,),
        in_specs=[
            pl.BlockSpec(triple.shape, lambda n: (0, 0)),
            pl.BlockSpec((near, rows, step), lambda n: (0, 0, n)),
        ],
        out_specs=[
            pl.BlockSpec((step, width), lambda n: (n, 0)),
            pl.BlockSpec((step, width), lambda n: (n, 0)),
            pl.BlockSpec((width, step), lambda n: (0, n)),
        ],
    )(later, plane)
    grad_inputs = call(add_pieces, shape((own, depth), BF16), (columns * own * depth, 2 * columns * own * depth))(pieces)
    return (grad_inputs, grad_gate_weight, grad_up_weight, grad_down_weight)


def solution(mesh):
    fine = Mesh(mesh.devices.reshape(2, 4, 4, 2, 4, 2), ("z_lo", "x", "z_hi", "core", "y_hi", "y_lo"))
    in_specs = (P(GROUP, ROW), P(GROUP, ROW), P(ROW, GROUP), P(ROW, GROUP), P(GROUP, ROW))
    out_specs = (P(GROUP, ROW), P(ROW, GROUP), P(ROW, GROUP), P(GROUP, ROW))
    return jax.shard_map(body, mesh=fine, in_specs=in_specs, out_specs=out_specs, check_vma=False)
```

```python
import jax
import jax.numpy as jnp
from jax import lax
from jax.experimental import pallas as pl
from jax.experimental.pallas import tpu as pltpu
from jax.sharding import Mesh
from jax.sharding import PartitionSpec as P

DP = ("x", "z_lo")
NEAR = ("x", "z_lo", "y_lo")
COLUMN = ("y_lo", "y_hi")
GROUP = ("z_lo", "x", "y_hi", "y_lo")
ROW = ("z_hi", "core")
FIRST_PAIRS = ((0, 1), (2, 3))
SECOND_PAIRS = ((0, 3), (1, 2))
MIB = 1024 * 1024
EXTRA = 8
TOP = 14
F16 = jnp.float16
F32 = jnp.float32
BF16 = jnp.bfloat16
LAST = (((1,), (1,)), ((), ()))
FIRST = (((0,), (0,)), ((), ()))


def exchange(pieces, axes):
    return lax.all_to_all(pieces, axes, split_axis=0, concat_axis=0, tiled=True)


def spread(block, axes):
    n = lax.axis_size(axes)
    return exchange(jnp.broadcast_to(block[None], (n,) + block.shape), axes)


def call(kernel, out_shape, cost, limit=20, **rest):
    flops, size = cost
    return pl.pallas_call(
        kernel,
        out_shape=out_shape,
        cost_estimate=pl.CostEstimate(flops=flops, bytes_accessed=size, transcendentals=0),
        compiler_params=pltpu.CompilerParams(vmem_limit_bytes=limit * MIB),
        **rest,
    )


def upper(shape):
    return lax.broadcasted_iota(jnp.int32, shape, len(shape) - 2) < 4


def split_line(line_ref, out_ref):
    columns, _, depth = line_ref.shape
    blocks = line_ref[...].astype(F32)
    top = upper((8, depth))
    inputs, cotangents = [], []
    for j in range(columns // 2):
        a, b = blocks[2 * j], blocks[2 * j + 1]
        inputs.append(jnp.where(top, a, pltpu.roll(b, 4, 0)))
        cotangents.append(jnp.where(top, pltpu.roll(a, 4, 0), b))
    rows = jnp.concatenate(inputs + cotangents, axis=0).astype(BF16)
    for p in range(out_ref.shape[0]):
        out_ref[p] = rows


def forward(plane_ref, gate_ref, up_ref, down_ref, out_ref):
    planes, rows, depth = plane_ref.shape
    half = rows // 2
    width = gate_ref.shape[1]
    inputs = plane_ref[:, :half, :].reshape(planes * half, depth)
    cotangents = plane_ref[:, half:, :].reshape(planes * half, depth)
    joined = jnp.concatenate([gate_ref[...], up_ref[...]], axis=1)
    out_ref[:, : 2 * width] = jnp.dot(inputs, joined, preferred_element_type=F32)
    out_ref[:, 2 * width :] = lax.dot_general(cotangents, down_ref[...], LAST, preferred_element_type=F32)


def store_scaled(pair, out_ref):
    tokens = pair.shape[0]
    largest = jnp.max(jnp.abs(pair), axis=0, keepdims=True)
    power = jnp.floor(jnp.log2(jnp.maximum(largest, 1e-30)))
    out_ref[:tokens, :] = pair * jnp.exp2(-power) * 2.0**TOP
    out_ref[tokens:, :] = jnp.broadcast_to(power, (EXTRA, pair.shape[1]))


def sum_scaled(parts_ref):
    tokens = parts_ref.shape[1] - EXTRA
    summed = 0.0
    for z in range(parts_ref.shape[0]):
        power = parts_ref[z, tokens:, :][:1]
        summed = summed + parts_ref[z, :tokens, :] * (jnp.exp2(power) * 2.0**-TOP)
    return summed


def scale_pair(core_ref, both_ref, out_ref):
    store_scaled(both_ref[0] + both_ref[1], out_ref)


def rescale(parts_ref, out_ref):
    store_scaled(sum_scaled(parts_ref), out_ref)


def activate(parts_ref, out_ref):
    width = out_ref.shape[1] // 3
    summed = jnp.concatenate([sum_scaled(parts_ref.at[:, c]) for c in range(2)], axis=0)
    gate = summed[:, :width]
    up = summed[:, width : 2 * width]
    hidden_grad = summed[:, 2 * width :]
    sigma = 1.0 / (1.0 + jnp.exp(-gate))
    active = gate * sigma
    out_ref[:, :width] = (active * up).astype(BF16)
    out_ref[:, width : 2 * width] = (hidden_grad * up * sigma * (1.0 + gate * (1.0 - sigma))).astype(BF16)
    out_ref[:, 2 * width :] = (hidden_grad * active).astype(BF16)


def input_grads(triple_ref, gate_ref, up_ref, out_ref):
    tokens = triple_ref.shape[0]
    depth, width = gate_ref.shape
    both = triple_ref[:, width:]
    step = 256
    for n in range(0, depth, step):
        joined = jnp.concatenate([gate_ref[n : n + step, :], up_ref[n : n + step, :]], axis=1)
        product = lax.dot_general(both, joined, LAST, preferred_element_type=F32)
        out_ref[:, :, n : n + step] = product.reshape(out_ref.shape[:2] + (step,)).astype(BF16)


def add_planes(pieces_ref, out_ref):
    _, rows, depth = pieces_ref.shape
    half = depth // 2
    total = pieces_ref[0].astype(F32)
    for p in range(1, pieces_ref.shape[0]):
        total = total + pieces_ref[p].astype(F32)
    left = total[:, :half].reshape(rows // 8, 8, half)
    right = total[:, half:].reshape(rows // 8, 8, half)
    top = upper(left.shape)
    out_ref[:, 0] = jnp.where(top, left, pltpu.roll(right, 4, 1)).astype(BF16)
    out_ref[:, 1] = jnp.where(top, pltpu.roll(left, 4, 1), right).astype(BF16)


def weight_grads(triple_ref, plane_ref, gate_ref, up_ref, down_ref):
    planes, rows, step = plane_ref.shape
    half = rows // 2
    width = gate_ref.shape[1]
    inputs = plane_ref[:, :half, :].reshape(planes * half, step)
    cotangents = plane_ref[:, half:, :].reshape(planes * half, step)
    both = lax.dot_general(inputs, triple_ref[:, width:], FIRST, preferred_element_type=F32)
    gate_ref[...] = both[:, :width].astype(BF16)
    up_ref[...] = both[:, width:].astype(BF16)
    hidden = triple_ref[:, :width]
    down_ref[...] = lax.dot_general(hidden, cotangents, FIRST, preferred_element_type=F32).astype(BF16)


def add_pieces(pieces_ref, out_ref):
    half = pieces_ref.shape[2]
    total = jnp.sum(pieces_ref[...].astype(F32), axis=0)
    out_ref[:, :half] = total[:4].astype(BF16)
    out_ref[:, half:] = pltpu.roll(total, 4, 0)[:4].astype(BF16)


def body(inputs, cotangent, gate_weight, up_weight, down_weight):
    own, depth = inputs.shape
    width = gate_weight.shape[1]
    columns = lax.axis_size(COLUMN)
    planes = lax.axis_size(DP)
    groups = columns * planes
    tokens = own * groups
    near = lax.axis_size(NEAR)
    rows = 2 * tokens // near
    shape = jax.ShapeDtypeStruct

    block = jnp.concatenate([inputs, cotangent], axis=0)
    core = lax.axis_index("core").astype(jnp.int32).reshape(1)
    block, core = lax.optimization_barrier((block, core))
    line = spread(block, "y_hi").reshape(groups // near, 2 * own, depth)
    copies = call(
        split_line,
        shape((near, rows, depth), BF16),
        (0, near * rows * depth * 2),
    )(line)
    plane = exchange(copies, NEAR).reshape(near, rows, depth)

    partial = call(
        forward,
        shape((tokens, 3 * width), F32),
        (6 * tokens * depth * width, plane.size * 2 + 6 * depth * width),
    )(plane, gate_weight, up_weight, down_weight)
    both = lax.all_gather(partial, "core", axis=0, tiled=False)
    half = tokens // 2
    scaled = call(
        scale_pair,
        shape((half + EXTRA, 3 * width), F32),
        (tokens * width * 10, tokens * width * 18),
        grid_spec=pltpu.PrefetchScalarGridSpec(
            num_scalar_prefetch=1,
            grid=(1,),
            in_specs=[pl.BlockSpec((2, half, 3 * width), lambda i, c: (0, c[0], 0))],
            out_specs=pl.BlockSpec((half + EXTRA, 3 * width), lambda i, c: (0, 0)),
        ),
    )(core, both).astype(F16)
    parts = lax.all_gather(scaled, "z_hi", axis=0, tiled=False, axis_index_groups=FIRST_PAIRS)
    scaled = call(rescale, shape(scaled.shape, F32), (tokens * width * 10, parts.size * 4))(parts.astype(F32)).astype(F16)
    quads = tuple(tuple(2 * z + c for z in pair for c in range(2)) for pair in SECOND_PAIRS)
    parts = lax.all_gather(scaled, ROW, axis=0, tiled=False, axis_index_groups=quads)
    parts = parts.reshape((2, 2) + scaled.shape)

    triple = call(activate, shape((tokens, 3 * width), BF16), (tokens * width * 20, parts.size * 4))(parts.astype(F32))

    partial_in = call(
        input_grads,
        shape((planes, columns * own, depth), BF16),
        (4 * tokens * depth * width, 2 * tokens * depth + 4 * depth * width),
    )(triple, gate_weight, up_weight)
    line_in = call(
        add_planes,
        shape((columns // 2, 2, 2 * own, depth // 2), BF16),
        (tokens * depth, 2 * tokens * depth),
    )(exchange(partial_in, DP))
    line_in, later = lax.optimization_barrier((line_in, triple))
    pieces = exchange(line_in.reshape(columns, 2 * own, depth // 2), COLUMN)
    step = depth // 4
    grad_gate_weight, grad_up_weight, grad_down_weight = call(
        weight_grads,
        [shape(w.shape, BF16) for w in (gate_weight, up_weight, down_weight)],
        (6 * tokens * depth * width, plane.size * 2 + 6 * depth * width),
        grid=(4,),
        in_specs=[
            pl.BlockSpec(triple.shape, lambda n: (0, 0)),
            pl.BlockSpec((near, rows, step), lambda n: (0, 0, n)),
        ],
        out_specs=[
            pl.BlockSpec((step, width), lambda n: (n, 0)),
            pl.BlockSpec((step, width), lambda n: (n, 0)),
            pl.BlockSpec((width, step), lambda n: (0, n)),
        ],
    )(later, plane)
    grad_inputs = call(add_pieces, shape((own, depth), BF16), (columns * own * depth, 2 * columns * own * depth))(pieces)
    return (grad_inputs, grad_gate_weight, grad_up_weight, grad_down_weight)


def solution(mesh):
    fine = Mesh(mesh.devices.reshape(2, 4, 4, 2, 4, 2), ("z_lo", "x", "z_hi", "core", "y_hi", "y_lo"))
    in_specs = (P(GROUP, ROW), P(GROUP, ROW), P(ROW, GROUP), P(ROW, GROUP), P(GROUP, ROW))
    out_specs = (P(GROUP, ROW), P(ROW, GROUP), P(ROW, GROUP), P(GROUP, ROW))
    return jax.shard_map(body, mesh=fine, in_specs=in_specs, out_specs=out_specs, check_vma=False)
```

```python
import jax
import jax.numpy as jnp
from jax import lax
from jax.experimental import pallas as pl
from jax.experimental.pallas import tpu as pltpu
from jax.sharding import Mesh
from jax.sharding import PartitionSpec as P

DP = ("x", "z_lo")
NEAR = ("x", "z_lo", "y_lo")
COLUMN = ("y_lo", "y_hi")
GROUP = ("z_lo", "x", "y_hi", "y_lo")
ROW = ("z_hi", "core")
FIRST_PAIRS = ((0, 1), (2, 3))
SECOND_PAIRS = ((0, 3), (1, 2))
MIB = 1024 * 1024
EXTRA = 8
TOP = 14
F16 = jnp.float16
F32 = jnp.float32
BF16 = jnp.bfloat16
LAST = (((1,), (1,)), ((), ()))
FIRST = (((0,), (0,)), ((), ()))


def exchange(pieces, axes):
    return lax.all_to_all(pieces, axes, split_axis=0, concat_axis=0, tiled=True)


def spread(block, axes):
    n = lax.axis_size(axes)
    return exchange(jnp.broadcast_to(block[None], (n,) + block.shape), axes)


def call(kernel, out_shape, cost, limit=20, **rest):
    flops, size = cost
    return pl.pallas_call(
        kernel,
        out_shape=out_shape,
        cost_estimate=pl.CostEstimate(flops=flops, bytes_accessed=size, transcendentals=0),
        compiler_params=pltpu.CompilerParams(vmem_limit_bytes=limit * MIB),
        **rest,
    )


def upper(shape):
    return lax.broadcasted_iota(jnp.int32, shape, len(shape) - 2) < 4


def split_line(line_ref, out_ref):
    columns, _, depth = line_ref.shape
    blocks = line_ref[...].astype(F32)
    top = upper((8, depth))
    inputs, cotangents = [], []
    for j in range(columns // 2):
        a, b = blocks[2 * j], blocks[2 * j + 1]
        inputs.append(jnp.where(top, a, pltpu.roll(b, 4, 0)))
        cotangents.append(jnp.where(top, pltpu.roll(a, 4, 0), b))
    rows = jnp.concatenate(inputs + cotangents, axis=0).astype(BF16)
    for p in range(out_ref.shape[0]):
        out_ref[p] = rows


def forward(plane_ref, gate_ref, up_ref, down_ref, out_ref):
    planes, rows, depth = plane_ref.shape
    half = rows // 2
    width = gate_ref.shape[1]
    inputs = plane_ref[:, :half, :].reshape(planes * half, depth)
    cotangents = plane_ref[:, half:, :].reshape(planes * half, depth)
    joined = jnp.concatenate([gate_ref[...], up_ref[...]], axis=1)
    out_ref[:, : 2 * width] = jnp.dot(inputs, joined, preferred_element_type=F32)
    out_ref[:, 2 * width :] = lax.dot_general(cotangents, down_ref[...], LAST, preferred_element_type=F32)


def store_scaled(pair, out_ref):
    tokens = pair.shape[0]
    largest = jnp.max(jnp.abs(pair), axis=0, keepdims=True)
    power = jnp.floor(jnp.log2(jnp.maximum(largest, 1e-30)))
    out_ref[:tokens, :] = pair * jnp.exp2(-power) * 2.0**TOP
    out_ref[tokens:, :] = jnp.broadcast_to(power, (EXTRA, pair.shape[1]))


def sum_scaled(parts_ref):
    tokens = parts_ref.shape[1] - EXTRA
    summed = 0.0
    for z in range(parts_ref.shape[0]):
        power = parts_ref[z, tokens:, :][:1]
        summed = summed + parts_ref[z, :tokens, :] * (jnp.exp2(power) * 2.0**-TOP)
    return summed


def scale_pair(core_ref, both_ref, out_ref):
    store_scaled(both_ref[0] + both_ref[1], out_ref)


def rescale(parts_ref, out_ref):
    store_scaled(sum_scaled(parts_ref), out_ref)


def activate(parts_ref, out_ref):
    width = out_ref.shape[1] // 3
    summed = jnp.concatenate([sum_scaled(parts_ref.at[:, c]) for c in range(2)], axis=0)
    gate = summed[:, :width]
    up = summed[:, width : 2 * width]
    hidden_grad = summed[:, 2 * width :]
    sigma = 1.0 / (1.0 + jnp.exp(-gate))
    active = gate * sigma
    out_ref[:, :width] = (active * up).astype(BF16)
    out_ref[:, width : 2 * width] = (hidden_grad * up * sigma * (1.0 + gate * (1.0 - sigma))).astype(BF16)
    out_ref[:, 2 * width :] = (hidden_grad * active).astype(BF16)


def input_grads(triple_ref, gate_ref, up_ref, out_ref):
    tokens = triple_ref.shape[0]
    depth, width = gate_ref.shape
    both = triple_ref[:, width:]
    step = 256
    for n in range(0, depth, step):
        joined = jnp.concatenate([gate_ref[n : n + step, :], up_ref[n : n + step, :]], axis=1)
        product = lax.dot_general(both, joined, LAST, preferred_element_type=F32)
        out_ref[:, :, n : n + step] = product.reshape(out_ref.shape[:2] + (step,)).astype(BF16)


def add_planes(pieces_ref, out_ref):
    _, rows, depth = pieces_ref.shape
    half = depth // 2
    total = pieces_ref[0].astype(F32)
    for p in range(1, pieces_ref.shape[0]):
        total = total + pieces_ref[p].astype(F32)
    left = total[:, :half].reshape(rows // 8, 8, half)
    right = total[:, half:].reshape(rows // 8, 8, half)
    top = upper(left.shape)
    out_ref[:, 0] = jnp.where(top, left, pltpu.roll(right, 4, 1)).astype(BF16)
    out_ref[:, 1] = jnp.where(top, pltpu.roll(left, 4, 1), right).astype(BF16)


def weight_grads(triple_ref, plane_ref, gate_ref, up_ref, down_ref):
    planes, rows, step = plane_ref.shape
    half = rows // 2
    width = gate_ref.shape[1]
    inputs = plane_ref[:, :half, :].reshape(planes * half, step)
    cotangents = plane_ref[:, half:, :].reshape(planes * half, step)
    both = lax.dot_general(inputs, triple_ref[:, width:], FIRST, preferred_element_type=F32)
    gate_ref[...] = both[:, :width].astype(BF16)
    up_ref[...] = both[:, width:].astype(BF16)
    hidden = triple_ref[:, :width]
    down_ref[...] = lax.dot_general(hidden, cotangents, FIRST, preferred_element_type=F32).astype(BF16)


def add_pieces(pieces_ref, out_ref):
    half = pieces_ref.shape[2]
    total = jnp.sum(pieces_ref[...].astype(F32), axis=0)
    out_ref[:, :half] = total[:4].astype(BF16)
    out_ref[:, half:] = pltpu.roll(total, 4, 0)[:4].astype(BF16)


def body(inputs, cotangent, gate_weight, up_weight, down_weight):
    own, depth = inputs.shape
    width = gate_weight.shape[1]
    columns = lax.axis_size(COLUMN)
    planes = lax.axis_size(DP)
    groups = columns * planes
    tokens = own * groups
    near = lax.axis_size(NEAR)
    rows = 2 * tokens // near
    shape = jax.ShapeDtypeStruct

    block = jnp.concatenate([inputs, cotangent], axis=0)
    core = lax.axis_index("core").astype(jnp.int32).reshape(1)
    block, core = lax.optimization_barrier((block, core))
    line = lax.all_gather(block, "y_hi", axis=0, tiled=False, axis_index_groups=FIRST_PAIRS)
    line = lax.all_gather(line, "y_hi", axis=0, tiled=True, axis_index_groups=SECOND_PAIRS)
    copies = call(
        split_line,
        shape((near, rows, depth), BF16),
        (0, near * rows * depth * 2),
    )(line)
    plane = exchange(copies, NEAR).reshape(near, rows, depth)

    partial = call(
        forward,
        shape((tokens, 3 * width), F32),
        (6 * tokens * depth * width, plane.size * 2 + 6 * depth * width),
    )(plane, gate_weight, up_weight, down_weight)
    both = lax.all_gather(partial, "core", axis=0, tiled=False)
    half = tokens // 2
    scaled = call(
        scale_pair,
        shape((half + EXTRA, 3 * width), F32),
        (tokens * width * 10, tokens * width * 18),
        grid_spec=pltpu.PrefetchScalarGridSpec(
            num_scalar_prefetch=1,
            grid=(1,),
            in_specs=[pl.BlockSpec((2, half, 3 * width), lambda i, c: (0, c[0], 0))],
            out_specs=pl.BlockSpec((half + EXTRA, 3 * width), lambda i, c: (0, 0)),
        ),
    )(core, both).astype(F16)
    parts = lax.all_gather(scaled, "z_hi", axis=0, tiled=False, axis_index_groups=FIRST_PAIRS)
    scaled = call(rescale, shape(scaled.shape, F32), (tokens * width * 10, parts.size * 4))(parts.astype(F32)).astype(F16)
    quads = tuple(tuple(2 * z + c for z in pair for c in range(2)) for pair in SECOND_PAIRS)
    parts = lax.all_gather(scaled, ROW, axis=0, tiled=False, axis_index_groups=quads)
    parts = parts.reshape((2, 2) + scaled.shape)

    triple = call(activate, shape((tokens, 3 * width), BF16), (tokens * width * 20, parts.size * 4))(parts.astype(F32))

    partial_in = call(
        input_grads,
        shape((planes, columns * own, depth), BF16),
        (4 * tokens * depth * width, 2 * tokens * depth + 4 * depth * width),
    )(triple, gate_weight, up_weight)
    line_in = call(
        add_planes,
        shape((columns // 2, 2, 2 * own, depth // 2), BF16),
        (tokens * depth, 2 * tokens * depth),
    )(exchange(partial_in, DP))
    line_in, later = lax.optimization_barrier((line_in, triple))
    pieces = exchange(line_in.reshape(columns, 2 * own, depth // 2), COLUMN)
    step = depth // 4
    grad_gate_weight, grad_up_weight, grad_down_weight = call(
        weight_grads,
        [shape(w.shape, BF16) for w in (gate_weight, up_weight, down_weight)],
        (6 * tokens * depth * width, plane.size * 2 + 6 * depth * width),
        grid=(4,),
        in_specs=[
            pl.BlockSpec(triple.shape, lambda n: (0, 0)),
            pl.BlockSpec((near, rows, step), lambda n: (0, 0, n)),
        ],
        out_specs=[
            pl.BlockSpec((step, width), lambda n: (n, 0)),
            pl.BlockSpec((step, width), lambda n: (n, 0)),
            pl.BlockSpec((width, step), lambda n: (0, n)),
        ],
    )(later, plane)
    grad_inputs = call(add_pieces, shape((own, depth), BF16), (columns * own * depth, 2 * columns * own * depth))(pieces)
    return (grad_inputs, grad_gate_weight, grad_up_weight, grad_down_weight)


def solution(mesh):
    fine = Mesh(mesh.devices.reshape(2, 4, 4, 2, 4, 2), ("z_lo", "x", "z_hi", "core", "y_hi", "y_lo"))
    in_specs = (P(GROUP, ROW), P(GROUP, ROW), P(ROW, GROUP), P(ROW, GROUP), P(GROUP, ROW))
    out_specs = (P(GROUP, ROW), P(ROW, GROUP), P(ROW, GROUP), P(GROUP, ROW))
    return jax.shard_map(body, mesh=fine, in_specs=in_specs, out_specs=out_specs, check_vma=False)
```
